128 devices in a mesh: island: 16 (over z_lo, x, core), fsdp: 8 (over y, z_hi).
Axes of the slice: x: 4, y: 4, z: 4 (z_hi: 2, z_lo: 2; z = z_hi * 2 + z_lo), core: 2. Of those that a mesh axis runs over, the one named last changes fastest.
Arguments:
- inner: float32 [16, 4, 256, 10240], P('island', None, 'fsdp'), may hold values from -24 to 24, as said below
- anchor: float32 [4, 256, 10240], P(None, 'fsdp'), may hold values from -100 to 100, as said below
- momentum: float32 [4, 256, 10240], P(None, 'fsdp'), may hold values from -3 to 3
Outputs:
- new_anchor: float32 [4, 256, 10240], P(None, 'fsdp')
- new_momentum: float32 [4, 256, 10240], P(None, 'fsdp')
The draws below stay inside these ranges and needn't reach their ends.
Inputs may be any that keep to these rules, and one draw needn't show every extreme that they name: `anchor`: finite values. `inner`: finite values.
All inputs are finite; a program needn't handle non-finite values.
Results may differ from the reference program's by a relative error of at most 0.00014.
Values sent between devices are 32-bit elements; how exact they have to be, the bound alone decides.
No kernel may reach another device: no remote copies, remote signals or barrier semaphores. Data moves between devices by JAX's collectives and lax.ppermute only.
A program may use at most 128 MiB of HBM per device.

```python
import math
import jax
import jax.numpy as jnp
from jax import lax

D = 10240
FRAG = 4
ROWS = 256
N_ISLAND = 16


def fragment_scale(key):
    order_key = jax.random.fold_in(key, 101)
    order = jax.random.permutation(order_key, 4)
    table = jnp.array([0.1, 0.11, 0.5, 1.0], jnp.float32)
    return table[order]


def draw_inner(key, part):
    scales = fragment_scale(key)
    key = jax.random.fold_in(key, 3)
    values = jnp.clip(4.0 * jax.random.normal(key, (N_ISLAND, FRAG, ROWS, D), jnp.float32), -24.0, 24.0)
    return values * scales[None, :, None, None]


def draw_anchor(key, part):
    scales = fragment_scale(key)
    key = jax.random.fold_in(key, 7)
    key_value, key_row, key_col = jax.random.split(key, 3)
    values = jnp.clip(jax.random.normal(key_value, (FRAG, ROWS, D), jnp.float32), -4.0, 4.0)
    position = jnp.arange(ROWS, dtype=jnp.float32) / ROWS
    row_scale = jnp.exp(math.log(10.0) * (position - 0.5))
    row_noise = jnp.exp(jax.random.uniform(key_row, (FRAG, ROWS), jnp.float32, -0.7, 0.7))
    col_scale = jnp.exp(jax.random.uniform(key_col, (FRAG, D), jnp.float32, -1.15, 1.15))
    shaped = values * (row_scale[None, :] * row_noise)[:, :, None] * col_scale[:, None, :]
    return shaped * scales[:, None, None]


def steps_of(stream_key, extent, shards, smallest, high):
    def one(dim, parts):
        draws = jax.random.uniform(jax.random.fold_in(jax.random.fold_in(stream_key, 6), dim), (parts,), jnp.float32, smallest / len(shards), high / len(shards))
        return jnp.repeat(jnp.exp(draws), extent[dim] // parts).reshape((-1,) + (1,) * (len(extent) - dim - 1))

    gain = one(*shards[0])
    for cut in shards[1:]:
        gain = gain * one(*cut)
    return gain


def centred(stream_key, shape, scale, reach, shards=(), kind=jnp.bfloat16):
    drawn = scale * jax.random.normal(stream_key, shape, jnp.float32)
    if shards:
        drawn = drawn * steps_of(stream_key, shape, shards, -0.22, 0.18)
    return jnp.clip(drawn, -reach, reach).astype(kind)


def setup_inputs(seed: int = 0) -> dict:
    arg_keys = jax.random.split(jax.random.key(seed), 4)
    return {
        "inner": draw_inner(jax.random.fold_in(arg_keys[3], 71), 0),
        "anchor": draw_anchor(jax.random.fold_in(arg_keys[3], 71), 0),
        "momentum": centred(arg_keys[2], (FRAG, ROWS, D), 0.5, 3.0, ((1, 8),), jnp.float32),
    }


EPS = 1e-06
RMS_MAX = 0.5
MU = 0.9
LR = 0.7

def reference(inner, anchor, momentum):
    average = lax.optimization_barrier(jnp.sum(anchor[None] - inner, axis=0)) / N_ISLAND
    mean_sq = lax.optimization_barrier(jnp.sum(average * average, axis=(1, 2))) / (ROWS * D)
    rms_value = jnp.sqrt(mean_sq + EPS)
    factor = jnp.minimum(1.0, RMS_MAX / rms_value)
    clipped = average * factor[:, None, None]
    new_momentum = MU * momentum + clipped
    new_anchor = anchor - LR * (clipped + MU * new_momentum)
    return (new_anchor, new_momentum)
```

```python
import jax
import jax.numpy as jnp
from jax import lax
from jax.sharding import PartitionSpec as P
from jax.experimental import pallas as pl
from jax.experimental.pallas import tpu as pltpu

EPS = 1e-06
RMS_MAX = 0.5
MU = 0.9
LR = 0.7
X, CORES = 4, 2


def island_id(z, x, core):
    return ((z % 2) * X + x % X) * CORES + core % CORES


def neighbour(x, core, parity):
    return x + 1 if (x + core + parity) % 2 == 0 else x - 1


PLACES = [(z, x, core) for z in range(2) for x in range(X) for core in range(CORES)]
CORE = [(island_id(*p), island_id(p[0], p[1], p[2] + 1)) for p in PLACES]
Z = [(island_id(*p), island_id(p[0] + 1, p[1], p[2])) for p in PLACES]
X0 = [(island_id(*p), island_id(p[0], neighbour(p[1], p[2], 0), p[2])) for p in PLACES]
X1 = [(island_id(*p), island_id(p[0], neighbour(p[1], p[2], 1), p[2])) for p in PLACES]
YZ = [(y, h) for y in range(4) for h in range(2)]
Y0 = [(y * 2 + h, (y ^ 1) * 2 + h) for y, h in YZ]
Y1 = [(y * 2 + h, ((y + (1 if y % 2 else -1)) % 4) * 2 + h) for y, h in YZ]
H = [(y * 2 + h, y * 2 + (1 - h)) for y, h in YZ]


def hop(value, pairs, axis="island"):
    return lax.ppermute(value, axis, pairs)


def update_kernel(cols, first, ids, scale, *refs):
    n = len(cols)
    sums = refs[:n]
    anchor, momentum = refs[n : n + 2]
    k = n + 2 + (0 if first else 2)
    out_a, out_m = refs[k : k + 2]
    va, vm = refs[k + 2 : k + 2 + n], refs[k + 2 + n : k + 2 + 2 * n]
    sem_in, sem_out = refs[k + 2 + 2 * n :]

    def place(ref, i):
        start, width = cols[i]
        return ref.at[ids[i], :, pl.ds(start, width)]

    loads, stores = [], []
    for i in range(n):
        loads.append(
            (
                pltpu.make_async_copy(place(anchor, i), va[i], sem_in.at[0, i]),
                pltpu.make_async_copy(place(momentum, i), vm[i], sem_in.at[1, i]),
            )
        )
        for copy in loads[-1]:
            copy.start()
    for i in range(n):
        for copy in loads[i]:
            copy.wait()
        factor = scale[ids[i]]
        clipped = sums[i][...] * factor
        new_m = MU * vm[i][...] + clipped
        va[i][...] = va[i][...] - LR * (clipped + MU * new_m)
        vm[i][...] = new_m
        out = (
            pltpu.make_async_copy(va[i], place(out_a, i), sem_out.at[0, i]),
            pltpu.make_async_copy(vm[i], place(out_m, i), sem_out.at[1, i]),
        )
        for copy in out:
            copy.start()
        stores.extend(out)
    for copy in stores:
        copy.wait()


def update(pieces, cols, ids, scale, anchor, momentum, outs=None):
    n = len(pieces)
    first = outs is None
    shape = jax.ShapeDtypeStruct(anchor.shape, anchor.dtype)
    any_spec = pl.BlockSpec(memory_space=pl.ANY)
    smem = pl.BlockSpec(memory_space=pltpu.SMEM)
    scratch = [pltpu.VMEM((32, w), jnp.float32) for _, w in cols] * 2
    total = sum(w for _, w in cols) * 32 * 4
    return pl.pallas_call(
        lambda *refs: update_kernel(cols, first, *refs),
        out_shape=(shape, shape),
        in_specs=[smem, smem]
        + [pl.BlockSpec(memory_space=pltpu.VMEM)] * n
        + [any_spec] * (2 if first else 4),
        out_specs=(any_spec, any_spec),
        scratch_shapes=scratch
        + [pltpu.SemaphoreType.DMA((2, n)), pltpu.SemaphoreType.DMA((2, n))],
        input_output_aliases={} if first else {n + 4: 0, n + 5: 1},
        compiler_params=pltpu.CompilerParams(vmem_limit_bytes=5 * total + (4 << 20)),
        cost_estimate=pl.CostEstimate(
            flops=2 * total, bytes_accessed=5 * total, transcendentals=0
        ),
    )(ids, scale, *pieces, anchor, momentum, *(() if first else outs))


WA, WB = 3456, 3456


def on_device(inner, anchor, momentum):
    inner = inner[0]
    rows, width = anchor.shape[1:]
    islands = lax.axis_size("island")
    entries = rows * lax.axis_size("fsdp") * width
    me = lax.axis_index("island")
    core, x, z = me % 2, (me // 2) % X, me // 8
    bit = ((x + 1 - core) // 2) % 2
    peer_bit = ((x + core) // 2) % 2
    a_cols, b_cols, c_cols = (0, WA), (WA, WB), (WA + WB, width - WA - WB)
    bc_cols = (WA, width - WA)

    def cut(array, frag, cols):
        return lax.dynamic_slice(array, (frag, 0, cols[0]), (1, rows, cols[1]))[0]

    own, other = 2 * core, 2 * (1 - core)
    got_a_out = hop(cut(inner, other + 1 - z, a_cols), CORE)
    got_bc_out = hop(cut(inner, other + 1 - peer_bit, bc_cols), CORE)
    got_a_in = hop(cut(inner, other + z, a_cols), CORE)
    got_bc_in = hop(cut(inner, other + peer_bit, bc_cols), CORE)

    def delta(got, frag, cols):
        base = cut(anchor, frag, cols)
        return (base - cut(inner, frag, cols)) + (base - got)

    a_r = hop(delta(got_a_out, own + 1 - z, a_cols), Z)
    bc_r = hop(delta(got_bc_out, own + 1 - bit, bc_cols), X0)
    a = delta(got_a_in, own + z, a_cols) + a_r
    bc = delta(got_bc_in, own + bit, bc_cols) + bc_r
    b, c = bc[:, :WB], bc[:, WB:]
    a_r, b_r, c_r = hop(a, X1), hop(b, X1), hop(c, Z)
    a, b, c = a + a_r, b + b_r, c + c_r
    a_r, b_r, c_r = hop(a, X0), hop(b, Z), hop(c, X1)
    a, bc = a + a_r, jnp.concatenate([b + b_r, c + c_r], axis=1)
    a_far, bc_far = hop(a, Z), hop(bc, X0)
    a_peer, bc_peer = hop(a, CORE), hop(bc, CORE)
    a_peer_far, bc_peer_far = hop(a_far, CORE), hop(bc_far, CORE)
    frag = jnp.arange(4)
    sq = jnp.where(frag == own + z, jnp.sum(a * a), 0.0)
    sq = sq + jnp.where(frag == own + bit, jnp.sum(bc * bc), 0.0)
    sq = jnp.broadcast_to(jnp.pad(sq, (0, 4))[:, None], (8, 128))
    for pairs, axis in ((X0, "island"), (Z, "island"), (CORE, "island"), (Y0, "fsdp"), (Y1, "fsdp"), (H, "fsdp")):
        sq = sq + hop(sq, pairs, axis)
    mean_sq = sq[:4, 0] * (0.5 / (islands * islands)) / entries
    factor = jnp.minimum(1.0, RMS_MAX / jnp.sqrt(mean_sq + EPS)) / islands
    cols = [a_cols, bc_cols, a_cols, bc_cols]
    near = jnp.stack([own + z, own + bit, other + z, other + peer_bit])
    far = jnp.stack([own + 1 - z, own + 1 - bit, other + 1 - z, other + 1 - peer_bit])
    outs = update([a, bc, a_peer, bc_peer], cols, near, factor, anchor, momentum)
    return tuple(
        update([a_far, bc_far, a_peer_far, bc_peer_far], cols, far, factor, anchor, momentum, outs)
    )


def solution(mesh):
    spec = P(None, "fsdp", None)
    return jax.shard_map(
        on_device,
        mesh=mesh,
        in_specs=(P("island", None, "fsdp", None), spec, spec),
        out_specs=(spec, spec),
        check_vma=False,
    )
```

```python
import jax
import jax.numpy as jnp
from jax import lax
from jax.sharding import PartitionSpec as P
from jax.experimental import pallas as pl
from jax.experimental.pallas import tpu as pltpu

EPS = 1e-06
RMS_MAX = 0.5
MU = 0.9
LR = 0.7
X, CORES = 4, 2


def island_id(z, x, core):
    return ((z % 2) * X + x % X) * CORES + core % CORES


def neighbour(x, core, parity):
    return x + 1 if (x + core + parity) % 2 == 0 else x - 1


PLACES = [(z, x, core) for z in range(2) for x in range(X) for core in range(CORES)]
CORE = [(island_id(*p), island_id(p[0], p[1], p[2] + 1)) for p in PLACES]
Z = [(island_id(*p), island_id(p[0] + 1, p[1], p[2])) for p in PLACES]
X0 = [(island_id(*p), island_id(p[0], neighbour(p[1], p[2], 0), p[2])) for p in PLACES]
X1 = [(island_id(*p), island_id(p[0], neighbour(p[1], p[2], 1), p[2])) for p in PLACES]
YZ = [(y, h) for y in range(4) for h in range(2)]
Y0 = [(y * 2 + h, (y ^ 1) * 2 + h) for y, h in YZ]
Y1 = [(y * 2 + h, ((y + (1 if y % 2 else -1)) % 4) * 2 + h) for y, h in YZ]
H = [(y * 2 + h, y * 2 + (1 - h)) for y, h in YZ]


def hop(value, pairs, axis="island"):
    return lax.ppermute(value, axis, pairs)


WA, WB = 3456, 3456
VMEM = pl.BlockSpec(memory_space=pltpu.VMEM)
SMEM = pl.BlockSpec(memory_space=pltpu.SMEM)
HBM = pl.BlockSpec(memory_space=pltpu.HBM)


def diagonal():
    pairs = []
    for z, x, core in PLACES:
        pairs.append((island_id(z, x, core), island_id(z + 1, neighbour(x, core, 0), core)))
    return pairs


ZX = diagonal()
FSDP_STEPS = ((Y0, "fsdp"), (Y1, "fsdp"), (H, "fsdp"))


def fetches(source, target, frag_a, frag_bc, sem):
    width = source.shape[2]
    return [
        pltpu.make_async_copy(source.at[frag_a, :, pl.ds(0, WA)], target.at[:, pl.ds(0, WA)], sem.at[0]),
        pltpu.make_async_copy(source.at[frag_bc, :, pl.ds(WA, width - WA)], target.at[:, pl.ds(WA, width - WA)], sem.at[1]),
    ]


def pick_kernel(ids, inner, send, keep, sem):
    copies = fetches(inner, send, ids[0], ids[1], sem.at[0]) + fetches(inner, keep, ids[2], ids[3], sem.at[1])
    for copy in copies:
        copy.start()
    for copy in copies:
        copy.wait()


def pick(ids, inner):
    rows, width = inner.shape[1:]
    shape = jax.ShapeDtypeStruct((rows, width), inner.dtype)
    return pl.pallas_call(
        pick_kernel,
        out_shape=(shape, shape),
        in_specs=[SMEM, HBM],
        out_specs=(VMEM, VMEM),
        scratch_shapes=[pltpu.SemaphoreType.DMA((2, 2))],
        compiler_params=pltpu.CompilerParams(vmem_limit_bytes=60 << 20),
        cost_estimate=pl.CostEstimate(flops=0, bytes_accessed=1024, transcendentals=0),
    )(ids, inner)


def differ_kernel(ids, inner, anchor, *refs):
    *outs, sem = refs
    groups = []
    for i in range(2):
        diff, base = outs[2 * i : 2 * i + 2]
        groups.append(
            fetches(inner, diff, ids[2 * i], ids[2 * i + 1], sem.at[i, 0])
            + fetches(anchor, base, ids[2 * i], ids[2 * i + 1], sem.at[i, 1])
        )
        for copy in groups[-1]:
            copy.start()
    for i in range(2):
        diff, base = outs[2 * i : 2 * i + 2]
        for copy in groups[i]:
            copy.wait()
        diff[...] = base[...] - diff[...]


def differ(ids, inner, anchor):
    rows, width = inner.shape[1:]
    shape = jax.ShapeDtypeStruct((rows, width), inner.dtype)
    return pl.pallas_call(
        differ_kernel,
        out_shape=(shape,) * 4,
        in_specs=[SMEM, HBM, HBM],
        out_specs=(VMEM,) * 4,
        scratch_shapes=[pltpu.SemaphoreType.DMA((2, 2, 2))],
        compiler_params=pltpu.CompilerParams(vmem_limit_bytes=50 << 20),
        cost_estimate=pl.CostEstimate(flops=0, bytes_accessed=1024, transcendentals=0),
    )(ids, inner, anchor)


def total_kernel(ids, a, b, c, a_r, b_r, c_r, near, bc, sq):
    width = near.shape[1]
    sums = []
    for mine, got, lo in ((a, a_r, 0), (b, b_r, WA), (c, c_r, WA + WB)):
        size = mine.shape[1]
        part = jnp.zeros((mine.shape[0], 128), jnp.float32)
        for start in range(0, size, 128):
            value = mine[:, start : start + 128] + got[:, start : start + 128]
            near[:, lo + start : lo + start + 128] = value
            if lo:
                bc[:, lo - WA + start : lo - WA + start + 128] = value
            part = part + value * value
        sums.append(part)
    row = lax.broadcasted_iota(jnp.int32, (8, 128), 0)
    left, right = jnp.sum(sums[0]), jnp.sum(sums[1] + sums[2])
    sq[...] = jnp.where(row == ids[0], left, 0.0) + jnp.where(row == ids[1], right, 0.0)


def total(ids, *pieces):
    rows = pieces[0].shape[0]
    width = sum(p.shape[1] for p in pieces[:3])
    shape = lambda *dims: jax.ShapeDtypeStruct(dims, jnp.float32)
    return pl.pallas_call(
        total_kernel,
        out_shape=(shape(rows, width), shape(rows, width - WA), shape(8, 128)),
        in_specs=[SMEM] + [VMEM] * 6,
        out_specs=(VMEM,) * 3,
        compiler_params=pltpu.CompilerParams(vmem_limit_bytes=12 << 20),
        cost_estimate=pl.CostEstimate(flops=0, bytes_accessed=1024, transcendentals=0),
    )(ids, *pieces)


def update_kernel(ids, scale, *refs):
    sums, (anchor, momentum, out_a, out_m, va, vm, sem_in, sem_out) = refs[:4], refs[4:]
    width = anchor.shape[2]
    chunks = []
    for i in range(4):
        for j, (lo, hi) in enumerate(((0, WA), (WA, width))):
            middle = lo + (hi - lo) // 256 * 128
            for start, stop in ((lo, middle), (middle, hi)):
                chunks.append((i, ids[2 * i + j], start, stop - start))

    def loads(n):
        i, frag, start, size = chunks[n]
        cols = pl.ds(start, size)
        return [
            pltpu.make_async_copy(anchor.at[frag, :, cols], va.at[i, :, cols], sem_in.at[0, n]),
            pltpu.make_async_copy(momentum.at[frag, :, cols], vm.at[i, :, cols], sem_in.at[1, n]),
        ]

    def stores(n):
        i, frag, start, size = chunks[n]
        cols = pl.ds(start, size)
        return [
            pltpu.make_async_copy(va.at[i, :, cols], out_a.at[frag, :, cols], sem_out.at[0, n]),
            pltpu.make_async_copy(vm.at[i, :, cols], out_m.at[frag, :, cols], sem_out.at[1, n]),
        ]

    for n in range(len(chunks)):
        for copy in loads(n):
            copy.start()
    for n, (i, frag, start, size) in enumerate(chunks):
        for copy in loads(n):
            copy.wait()
        cols = slice(start, start + size)
        clipped = sums[i][:, cols] * scale[frag]
        new_m = MU * vm[i, :, cols] + clipped
        va[i, :, cols] = va[i, :, cols] - LR * (clipped + MU * new_m)
        vm[i, :, cols] = new_m
        for copy in stores(n):
            copy.start()
    for n in range(len(chunks)):
        for copy in stores(n):
            copy.wait()


def update(pieces, ids, scale, anchor, momentum):
    shape = jax.ShapeDtypeStruct(anchor.shape, anchor.dtype)
    total = anchor.size * 4
    any_spec = pl.BlockSpec(memory_space=pl.ANY)
    return pl.pallas_call(
        update_kernel,
        out_shape=(shape, shape),
        in_specs=[SMEM, SMEM] + [VMEM] * 4 + [any_spec] * 2,
        out_specs=(HBM, HBM),
        scratch_shapes=[pltpu.VMEM(anchor.shape, jnp.float32)] * 2 + [pltpu.SemaphoreType.DMA((2, 16))] * 2,
        compiler_params=pltpu.CompilerParams(vmem_limit_bytes=56 << 20),
        cost_estimate=pl.CostEstimate(flops=2 * total, bytes_accessed=5 * total, transcendentals=0),
    )(ids, scale, *pieces, anchor, momentum)


def on_device(inner, anchor, momentum):
    inner = inner[0]
    rows, width = anchor.shape[1:]
    islands = lax.axis_size("island")
    entries = rows * 8 * width
    me = lax.axis_index("island").astype(jnp.uint32)
    core, x, z = me % 2, (me // 2) % X, me // 8
    bit, peer_bit = ((x + 1 - core) // 2) % 2, ((x + core) // 2) % 2
    core, z, bit, peer_bit = (v.astype(jnp.int32) for v in (core, z, bit, peer_bit))
    own, other = 2 * core, 2 * (1 - core)
    order = []

    def turn(value):
        return lax.optimization_barrier((value, order[-1]))[0] if order else value

    def note(value):
        order.append(value)
        return value

    far_own, near_own = (own + 1 - z, own + 1 - bit), (own + z, own + bit)
    far_other, near_other = (other + 1 - z, other + 1 - peer_bit), (other + z, other + peer_bit)
    send, keep = pick(jnp.stack(far_other + near_other), inner)
    got_send = hop(send, CORE)
    got_keep = hop(keep, CORE)
    diff_send, base_send, diff_keep, base_keep = differ(jnp.stack(far_own + near_own), inner, anchor)
    send = diff_send + (base_send - got_send)
    a_r, bc_r = hop(send[:, :WA], Z), hop(send[:, WA:], X0)
    note(send)
    kept = note(diff_keep + (base_keep - turn(got_keep)))
    a = turn(a_r) + kept[:, :WA]
    bc = turn(bc_r) + kept[:, WA:]
    b, c = bc[:, :WB], bc[:, WB:]
    ab = note(jnp.concatenate([a, b], axis=1))
    c_r, ab_r = hop(c, Z), hop(ab, X1)
    c = note(turn(c_r) + c)
    ab = note(turn(ab_r) + ab)
    a, b = ab[:, :WA], ab[:, WA:]
    b_r, a_r, c_r = hop(b, Z), hop(a, X0), hop(c, X1)
    near, bc, sq = total(jnp.stack(near_own), a, b, c, a_r, b_r, c_r)
    note(sq)
    steps = ((ZX, "island"), (CORE, "island")) + FSDP_STEPS
    for k, step in enumerate(steps):
        sq = note(sq + turn(hop(sq, *step)))
        if k == 0:
            a_far, bc_far = hop(turn(near)[:, :WA], Z), hop(turn(bc), X0)
        if k == 1:
            near_peer = hop(turn(near), CORE)
        if k == 3:
            far = jnp.concatenate([turn(v) for v in (a_far, bc_far)], axis=1)
            far_peer = hop(far, CORE)
            note(far)
    mean_sq = sq[:4, 0] * (1.0 / (islands * islands)) / entries
    factor = jnp.minimum(1.0, RMS_MAX / jnp.sqrt(mean_sq + EPS)) / islands
    ids = jnp.stack(near_own + near_other + far_own + far_other)
    return tuple(update([near, near_peer, far, far_peer], ids, factor, anchor, momentum))


def solution(mesh):
    spec = P(None, "fsdp", None)
    return jax.shard_map(
        on_device,
        mesh=mesh,
        in_specs=(P("island", None, "fsdp", None), spec, spec),
        out_specs=(spec, spec),
        check_vma=False,
    )
```

```python
import jax
import jax.numpy as jnp
from jax import lax
from jax.sharding import PartitionSpec as P
from jax.experimental import pallas as pl
from jax.experimental.pallas import tpu as pltpu

EPS = 1e-06
RMS_MAX = 0.5
MU = 0.9
LR = 0.7
X, CORES = 4, 2


def island_id(z, x, core):
    return ((z % 2) * X + x % X) * CORES + core % CORES


def neighbour(x, core, parity):
    return x + 1 if (x + core + parity) % 2 == 0 else x - 1


PLACES = [(z, x, core) for z in range(2) for x in range(X) for core in range(CORES)]
CORE = [(island_id(*p), island_id(p[0], p[1], p[2] + 1)) for p in PLACES]
Z = [(island_id(*p), island_id(p[0] + 1, p[1], p[2])) for p in PLACES]
X0 = [(island_id(*p), island_id(p[0], neighbour(p[1], p[2], 0), p[2])) for p in PLACES]
X1 = [(island_id(*p), island_id(p[0], neighbour(p[1], p[2], 1), p[2])) for p in PLACES]
YZ = [(y, h) for y in range(4) for h in range(2)]
Y0 = [(y * 2 + h, (y ^ 1) * 2 + h) for y, h in YZ]
Y1 = [(y * 2 + h, ((y + (1 if y % 2 else -1)) % 4) * 2 + h) for y, h in YZ]
H = [(y * 2 + h, y * 2 + (1 - h)) for y, h in YZ]


def hop(value, pairs, axis="island"):
    return lax.ppermute(value, axis, pairs)


WA, WB = 3456, 3456
VMEM = pl.BlockSpec(memory_space=pltpu.VMEM)
SMEM = pl.BlockSpec(memory_space=pltpu.SMEM)
HBM = pl.BlockSpec(memory_space=pltpu.HBM)


def diagonal():
    pairs = []
    for z, x, core in PLACES:
        pairs.append((island_id(z, x, core), island_id(z + 1, x + 2, core)))
    return pairs


ZX = diagonal()
FSDP_STEPS = ((Y0, "fsdp"), (Y1, "fsdp"), (H, "fsdp"))


def position():
    me = lax.axis_index("island")
    core, x, z = me & 1, (me >> 1) & (X - 1), me >> 3
    return core, z, ((x + 1 - core) >> 1) & 1, ((x + core) >> 1) & 1


def fragments(mine, kept):
    core, z, bit, peer_bit = position()
    flip = 0 if kept else 1
    if mine:
        return 2 * core + (z ^ flip), 2 * core + (bit ^ flip)
    return 2 * (1 - core) + (z ^ flip), 2 * (1 - core) + (peer_bit ^ flip)


def fetches(source, target, frags, sem):
    rows, width = source.shape[1:]
    copies = []
    for k in range(rows // 8):
        for j, (lo, size) in enumerate(((0, WA), (WA, width - WA))):
            block = (pl.ds(8 * k, 8), pl.ds(lo, size))
            copies.append(pltpu.make_async_copy(source.at[(frags[j], *block)], target.at[block], sem.at[2 * k + j]))
    return copies


def pick_kernel(kept, inner, out, sem):
    copies = fetches(inner, out, fragments(False, kept), sem)
    for copy in copies:
        copy.start()
    for copy in copies:
        copy.wait()


def pick(kept, inner):
    rows, width = inner.shape[1:]
    return pl.pallas_call(
        lambda *refs: pick_kernel(kept, *refs),
        out_shape=jax.ShapeDtypeStruct((rows, width), inner.dtype),
        in_specs=[HBM],
        out_specs=VMEM,
        scratch_shapes=[pltpu.SemaphoreType.DMA((8,))],
        compiler_params=pltpu.CompilerParams(vmem_limit_bytes=(44 if kept else 48) << 20),
        cost_estimate=pl.CostEstimate(flops=0, bytes_accessed=1024, transcendentals=0),
    )(inner)


def differ_kernel(kept, inner, anchor, diff, base, sem):
    frags = fragments(True, kept)
    copies = fetches(inner, diff, frags, sem.at[0]) + fetches(anchor, base, frags, sem.at[1])
    for copy in copies:
        copy.start()
    for copy in copies:
        copy.wait()
    for start in range(0, diff.shape[1], 128):
        cols = slice(start, start + 128)
        diff[:, cols] = base[:, cols] - diff[:, cols]


def differ(kept, inner, anchor):
    rows, width = inner.shape[1:]
    shape = jax.ShapeDtypeStruct((rows, width), inner.dtype)
    return pl.pallas_call(
        lambda *refs: differ_kernel(kept, *refs),
        out_shape=(shape, shape),
        in_specs=[HBM, HBM],
        out_specs=(VMEM, VMEM),
        scratch_shapes=[pltpu.SemaphoreType.DMA((2, 8))],
        compiler_params=pltpu.CompilerParams(vmem_limit_bytes=(44 if kept else 48) << 20),
        cost_estimate=pl.CostEstimate(flops=0, bytes_accessed=1024, transcendentals=0),
    )(inner, anchor)


def first_kernel(diff, base, got, a_r, bc_r, ab, c):
    for start in range(0, diff.shape[1], 128):
        cols = slice(start, start + 128)
        far = a_r[:, cols] if start < WA else bc_r[:, start - WA : start - WA + 128]
        value = diff[:, cols] + (base[:, cols] - got[:, cols]) + far
        if start < WA + WB:
            ab[:, cols] = value
        else:
            c[:, start - WA - WB : start - WA - WB + 128] = value


def second_kernel(ab, c, ab_r, c_r, a_out, b_out, c_out):
    for start in range(0, ab.shape[1], 128):
        cols = slice(start, start + 128)
        out, at = (a_out, start) if start < WA else (b_out, start - WA)
        out[:, at : at + 128] = ab[:, cols] + ab_r[:, cols]
    c_out[...] = c[...] + c_r[...]


def in_vmem(kernel, widths, *arrays):
    shapes = [jax.ShapeDtypeStruct((arrays[0].shape[0], w), jnp.float32) for w in widths]
    return pl.pallas_call(
        kernel,
        out_shape=tuple(shapes),
        in_specs=[VMEM] * len(arrays),
        out_specs=(VMEM,) * len(widths),
        compiler_params=pltpu.CompilerParams(vmem_limit_bytes=16 << 20),
        cost_estimate=pl.CostEstimate(flops=0, bytes_accessed=1024, transcendentals=0),
    )(*arrays)


def total_kernel(a, b, c, a_r, b_r, c_r, near, bc, sq):
    frags = fragments(True, True)
    sums = []
    for mine, got, lo in ((a, a_r, 0), (b, b_r, WA), (c, c_r, WA + WB)):
        size = mine.shape[1]
        part = jnp.zeros((mine.shape[0], 128), jnp.float32)
        for start in range(0, size, 128):
            value = mine[:, start : start + 128] + got[:, start : start + 128]
            near[:, lo + start : lo + start + 128] = value
            if lo:
                bc[:, lo - WA + start : lo - WA + start + 128] = value
            part = part + value * value
        sums.append(part)
    row = lax.broadcasted_iota(jnp.int32, (8, 128), 0)
    left, right = jnp.sum(sums[0]), jnp.sum(sums[1] + sums[2])
    sq[...] = jnp.where(row == frags[0], left, 0.0) + jnp.where(row == frags[1], right, 0.0)


def total(*pieces):
    rows = pieces[0].shape[0]
    width = sum(p.shape[1] for p in pieces[:3])
    shape = lambda *dims: jax.ShapeDtypeStruct(dims, jnp.float32)
    return pl.pallas_call(
        total_kernel,
        out_shape=(shape(rows, width), shape(rows, width - WA), shape(8, 128)),
        in_specs=[VMEM] * 6,
        out_specs=(VMEM,) * 3,
        compiler_params=pltpu.CompilerParams(vmem_limit_bytes=12 << 20),
        cost_estimate=pl.CostEstimate(flops=0, bytes_accessed=1024, transcendentals=0),
    )(*pieces)


def update_kernel(entries, islands, sq, *refs):
    sums, (anchor, momentum, out_a, out_m, va, vm, sem_in, sem_out) = refs[:4], refs[4:]
    width = anchor.shape[2]
    frags = [fragments(*which) for which in ((True, True), (False, True), (True, False), (False, False))]
    chunks = []
    for i in range(4):
        for j, (lo, hi) in enumerate(((0, WA), (WA, width))):
            middle = lo + (hi - lo) // 256 * 128
            for start, stop in ((lo, middle), (middle, hi)):
                chunks.append((i, frags[i][j], start, stop - start))

    def loads(n):
        i, frag, start, size = chunks[n]
        cols = pl.ds(start, size)
        return [
            pltpu.make_async_copy(anchor.at[frag, :, cols], va.at[i, :, cols], sem_in.at[0, n]),
            pltpu.make_async_copy(momentum.at[frag, :, cols], vm.at[i, :, cols], sem_in.at[1, n]),
        ]

    def stores(n):
        i, frag, start, size = chunks[n]
        cols = pl.ds(start, size)
        return [
            pltpu.make_async_copy(va.at[i, :, cols], out_a.at[frag, :, cols], sem_out.at[0, n]),
            pltpu.make_async_copy(vm.at[i, :, cols], out_m.at[frag, :, cols], sem_out.at[1, n]),
        ]

    for n in range(len(chunks)):
        for copy in loads(n):
            copy.start()
    for n, (i, frag, start, size) in enumerate(chunks):
        mean_sq = jnp.broadcast_to(sq[pl.ds(frag, 1), :], (8, 128)) * (1.0 / (islands * islands)) / entries
        factor = jnp.minimum(1.0, RMS_MAX / jnp.sqrt(mean_sq + EPS)) / islands
        for copy in loads(n):
            copy.wait()
        for at in range(start, start + size, 128):
            for row in range(0, 32, 8):
                block = (slice(row, row + 8), slice(at, at + 128))
                clipped = sums[i][block] * factor
                new_m = MU * vm[(i, *block)] + clipped
                va[(i, *block)] = va[(i, *block)] - LR * (clipped + MU * new_m)
                vm[(i, *block)] = new_m
        for copy in stores(n):
            copy.start()
    for n in range(len(chunks)):
        for copy in stores(n):
            copy.wait()


def update(sq, pieces, anchor, momentum, entries, islands):
    shape = jax.ShapeDtypeStruct(anchor.shape, anchor.dtype)
    total = anchor.size * 4
    any_spec = pl.BlockSpec(memory_space=pl.ANY)
    return pl.pallas_call(
        lambda *refs: update_kernel(entries, islands, *refs),
        out_shape=(shape, shape),
        in_specs=[VMEM] * 5 + [any_spec] * 2,
        out_specs=(HBM, HBM),
        scratch_shapes=[pltpu.VMEM(anchor.shape, jnp.float32)] * 2 + [pltpu.SemaphoreType.DMA((2, 16))] * 2,
        compiler_params=pltpu.CompilerParams(vmem_limit_bytes=40 << 20),
        cost_estimate=pl.CostEstimate(flops=2 * total, bytes_accessed=5 * total, transcendentals=0),
    )(sq, *pieces, anchor, momentum)


def on_device(inner, anchor, momentum):
    inner = inner[0]
    rows, width = anchor.shape[1:]
    islands = lax.axis_size("island")
    entries = rows * 8 * width
    order = []

    def turn(value):
        return lax.optimization_barrier((value, order[-1]))[0] if order else value

    def note(value):
        order.append(value)
        return value

    got_send = hop(pick(False, inner), CORE)
    diff_send, base_send = differ(False, inner, anchor)
    send = note(diff_send + (base_send - got_send))
    got_keep = hop(pick(True, turn(inner)), CORE)
    diff_keep, base_keep = differ(True, turn(inner), anchor)
    a_r, bc_r = hop(send[:, :WA], Z), hop(send[:, WA:], X0)
    ab, c = in_vmem(first_kernel, (WA + WB, width - WA - WB), diff_keep, base_keep, got_keep, a_r, bc_r)
    c_r, ab_r = hop(c, Z), hop(ab, X1)
    a, b, c = in_vmem(second_kernel, (WA, WB, width - WA - WB), ab, c, ab_r, c_r)
    b_r, a_r, c_r = hop(b, Z), hop(a, X0), hop(c, X1)
    near, bc, sq = total(a, b, c, a_r, b_r, c_r)
    note(sq)
    a_far, bc_far = hop(near[:, :WA], Z), hop(bc, X0)
    for k, step in enumerate(STEPS):
        if k == 1:
            near_peer = hop(turn(near), CORE)
        if k == 3:
            far = jnp.concatenate([turn(v) for v in (a_far, bc_far)], axis=1)
            far_peer = hop(far, CORE)
            note(far)
        sq = note(sq + turn(hop(turn(sq), *step)))
    return tuple(update(sq, [near, near_peer, far, far_peer], anchor, momentum, entries, islands))


STEPS = (*FSDP_STEPS[:2], (CORE, "island"), FSDP_STEPS[2], (ZX, "island"))


def solution(mesh):
    spec = P(None, "fsdp", None)
    return jax.shard_map(
        on_device,
        mesh=mesh,
        in_specs=(P("island", None, "fsdp", None), spec, spec),
        out_specs=(spec, spec),
        check_vma=False,
    )
```

```python
import jax
import jax.numpy as jnp
from jax import lax
from jax.sharding import PartitionSpec as P
from jax.experimental import pallas as pl
from jax.experimental.pallas import tpu as pltpu

EPS = 1e-06
RMS_MAX = 0.5
MU = 0.9
LR = 0.7
X, CORES = 4, 2


def island_id(z, x, core):
    return ((z % 2) * X + x % X) * CORES + core % CORES


def neighbour(x, core, parity):
    return x + 1 if (x + core + parity) % 2 == 0 else x - 1


PLACES = [(z, x, core) for z in range(2) for x in range(X) for core in range(CORES)]
CORE = [(island_id(*p), island_id(p[0], p[1], p[2] + 1)) for p in PLACES]
Z = [(island_id(*p), island_id(p[0] + 1, p[1], p[2])) for p in PLACES]
X0 = [(island_id(*p), island_id(p[0], neighbour(p[1], p[2], 0), p[2])) for p in PLACES]
X1 = [(island_id(*p), island_id(p[0], neighbour(p[1], p[2], 1), p[2])) for p in PLACES]
YZ = [(y, h) for y in range(4) for h in range(2)]
Y0 = [(y * 2 + h, (y ^ 1) * 2 + h) for y, h in YZ]
Y1 = [(y * 2 + h, ((y + (1 if y % 2 else -1)) % 4) * 2 + h) for y, h in YZ]
ZZ = [
    (island_id(z, x, core) * 8 + y * 2 + h, island_id(z + 1, x, core) * 8 + y * 2 + 1 - h)
    for z, x, core in PLACES
    for y, h in YZ
]


def hop(value, pairs, axis="island"):
    return lax.ppermute(value, axis, pairs)


WA, WB = 3456, 3456
VMEM = pl.BlockSpec(memory_space=pltpu.VMEM)
SMEM = pl.BlockSpec(memory_space=pltpu.SMEM)
HBM = pl.BlockSpec(memory_space=pltpu.HBM)


def diagonal():
    pairs = []
    for z, x, core in PLACES:
        pairs.append((island_id(z, x, core), island_id(z + 1, x + 2, core)))
    return pairs


ZX = diagonal()
FSDP_STEPS = ((Y0, "fsdp"), (Y1, "fsdp"), (ZZ, ("island", "fsdp")))


def position():
    me = lax.axis_index("island")
    core, x, z = me & 1, (me >> 1) & (X - 1), me >> 3
    return core, z, ((x + 1 - core) >> 1) & 1, ((x + core) >> 1) & 1


def fragments(mine, kept):
    core, z, bit, peer_bit = position()
    flip = 0 if kept else 1
    if mine:
        return 2 * core + (z ^ flip), 2 * core + (bit ^ flip)
    return 2 * (1 - core) + (z ^ flip), 2 * (1 - core) + (peer_bit ^ flip)


def fetches(source, target, frags, sem):
    rows, width = source.shape[1:]
    copies = []
    for k in range(rows // 8):
        for j, (lo, size) in enumerate(((0, WA), (WA, width - WA))):
            block = (pl.ds(8 * k, 8), pl.ds(lo, size))
            copies.append(pltpu.make_async_copy(source.at[(frags[j], *block)], target.at[block], sem.at[2 * k + j]))
    return copies


def pick_kernel(inner, send, keep, sem):
    copies = fetches(inner, send, fragments(False, False), sem.at[0])
    copies += fetches(inner, keep, fragments(False, True), sem.at[1])
    for copy in copies:
        copy.start()
    for copy in copies:
        copy.wait()


def pick(inner):
    rows, width = inner.shape[1:]
    shape = jax.ShapeDtypeStruct((rows, width), inner.dtype)
    return pl.pallas_call(
        pick_kernel,
        out_shape=(shape, shape),
        in_specs=[HBM],
        out_specs=(VMEM, VMEM),
        scratch_shapes=[pltpu.SemaphoreType.DMA((2, 8))],
        compiler_params=pltpu.CompilerParams(vmem_limit_bytes=48 << 20),
        cost_estimate=pl.CostEstimate(flops=0, bytes_accessed=1024, transcendentals=0),
    )(inner)


def differ_kernel(kept, inner, anchor, diff, base, sem):
    frags = fragments(True, kept)
    copies = fetches(inner, diff, frags, sem.at[0]) + fetches(anchor, base, frags, sem.at[1])
    for copy in copies:
        copy.start()
    for copy in copies:
        copy.wait()
    for start in range(0, diff.shape[1], 128):
        cols = slice(start, start + 128)
        diff[:, cols] = base[:, cols] - diff[:, cols]


def differ(kept, inner, anchor):
    rows, width = inner.shape[1:]
    shape = jax.ShapeDtypeStruct((rows, width), inner.dtype)
    return pl.pallas_call(
        lambda *refs: differ_kernel(kept, *refs),
        out_shape=(shape, shape),
        in_specs=[HBM, HBM],
        out_specs=(VMEM, VMEM),
        scratch_shapes=[pltpu.SemaphoreType.DMA((2, 8))],
        compiler_params=pltpu.CompilerParams(vmem_limit_bytes=(44 if kept else 48) << 20),
        cost_estimate=pl.CostEstimate(flops=0, bytes_accessed=1024, transcendentals=0),
    )(inner, anchor)


def first_kernel(diff, base, got, a_r, bc_r, ab, c):
    for start in range(0, diff.shape[1], 128):
        cols = slice(start, start + 128)
        far = a_r[:, cols] if start < WA else bc_r[:, start - WA : start - WA + 128]
        value = diff[:, cols] + (base[:, cols] - got[:, cols]) + far
        if start < WA + WB:
            ab[:, cols] = value
        else:
            c[:, start - WA - WB : start - WA - WB + 128] = value


def second_kernel(ab, c, ab_r, c_r, a_out, b_out, c_out):
    for start in range(0, ab.shape[1], 128):
        cols = slice(start, start + 128)
        out, at = (a_out, start) if start < WA else (b_out, start - WA)
        out[:, at : at + 128] = ab[:, cols] + ab_r[:, cols]
    c_out[...] = c[...] + c_r[...]


def in_vmem(kernel, widths, *arrays):
    shapes = [jax.ShapeDtypeStruct((arrays[0].shape[0], w), jnp.float32) for w in widths]
    return pl.pallas_call(
        kernel,
        out_shape=tuple(shapes),
        in_specs=[VMEM] * len(arrays),
        out_specs=(VMEM,) * len(widths),
        compiler_params=pltpu.CompilerParams(vmem_limit_bytes=16 << 20),
        cost_estimate=pl.CostEstimate(flops=0, bytes_accessed=1024, transcendentals=0),
    )(*arrays)


def total_kernel(a, b, c, a_r, b_r, c_r, near, bc, sq):
    frags = fragments(True, True)
    sums = []
    for mine, got, lo in ((a, a_r, 0), (b, b_r, WA), (c, c_r, WA + WB)):
        size = mine.shape[1]
        part = jnp.zeros((mine.shape[0], 128), jnp.float32)
        for start in range(0, size, 128):
            value = mine[:, start : start + 128] + got[:, start : start + 128]
            near[:, lo + start : lo + start + 128] = value
            if lo:
                bc[:, lo - WA + start : lo - WA + start + 128] = value
            part = part + value * value
        sums.append(part)
    row = lax.broadcasted_iota(jnp.int32, (8, 128), 0)
    left, right = jnp.sum(sums[0]), jnp.sum(sums[1] + sums[2])
    sq[...] = jnp.where(row == frags[0], left, 0.0) + jnp.where(row == frags[1], right, 0.0)


def total(*pieces):
    rows = pieces[0].shape[0]
    width = sum(p.shape[1] for p in pieces[:3])
    shape = lambda *dims: jax.ShapeDtypeStruct(dims, jnp.float32)
    return pl.pallas_call(
        total_kernel,
        out_shape=(shape(rows, width), shape(rows, width - WA), shape(8, 128)),
        in_specs=[VMEM] * 6,
        out_specs=(VMEM,) * 3,
        compiler_params=pltpu.CompilerParams(vmem_limit_bytes=12 << 20),
        cost_estimate=pl.CostEstimate(flops=0, bytes_accessed=1024, transcendentals=0),
    )(*pieces)


def update_kernel(entries, islands, sq, *refs):
    sums, (anchor, momentum, out_a, out_m, va, vm, sem_in, sem_out) = refs[:4], refs[4:]
    width = anchor.shape[2]
    frags = [fragments(*which) for which in ((True, True), (False, True), (True, False), (False, False))]
    chunks = []
    for i in range(4):
        for j, (lo, hi) in enumerate(((0, WA), (WA, width))):
            chunks.append((i, frags[i][j], lo, hi - lo))

    def loads(n):
        i, frag, start, size = chunks[n]
        cols = pl.ds(start, size)
        return [
            pltpu.make_async_copy(anchor.at[frag, :, cols], va.at[i, :, cols], sem_in.at[0, n]),
            pltpu.make_async_copy(momentum.at[frag, :, cols], vm.at[i, :, cols], sem_in.at[1, n]),
        ]

    def stores(n):
        i, frag, start, size = chunks[n]
        cols = pl.ds(start, size)
        return [
            pltpu.make_async_copy(va.at[i, :, cols], out_a.at[frag, :, cols], sem_out.at[0, n]),
            pltpu.make_async_copy(vm.at[i, :, cols], out_m.at[frag, :, cols], sem_out.at[1, n]),
        ]

    for n in range(len(chunks)):
        for copy in loads(n):
            copy.start()
    for n, (i, frag, start, size) in enumerate(chunks):
        mean_sq = jnp.broadcast_to(sq[pl.ds(frag, 1), :], (8, 128)) * (1.0 / (islands * islands)) / entries
        factor = jnp.minimum(1.0, RMS_MAX / jnp.sqrt(mean_sq + EPS)) / islands
        for copy in loads(n):
            copy.wait()
        for at in range(start, start + size, 128):
            for row in range(0, 32, 8):
                block = (slice(row, row + 8), slice(at, at + 128))
                clipped = sums[i][block] * factor
                new_m = MU * vm[(i, *block)] + clipped
                va[(i, *block)] = va[(i, *block)] - LR * (clipped + MU * new_m)
                vm[(i, *block)] = new_m
        for copy in stores(n):
            copy.start()
    for n in range(len(chunks)):
        for copy in stores(n):
            copy.wait()


def update(sq, pieces, anchor, momentum, entries, islands):
    shape = jax.ShapeDtypeStruct(anchor.shape, anchor.dtype)
    total = anchor.size * 4
    any_spec = pl.BlockSpec(memory_space=pl.ANY)
    return pl.pallas_call(
        lambda *refs: update_kernel(entries, islands, *refs),
        out_shape=(shape, shape),
        in_specs=[VMEM] * 5 + [any_spec] * 2,
        out_specs=(HBM, HBM),
        scratch_shapes=[pltpu.VMEM(anchor.shape, jnp.float32)] * 2 + [pltpu.SemaphoreType.DMA((2, 8))] * 2,
        compiler_params=pltpu.CompilerParams(vmem_limit_bytes=40 << 20),
        cost_estimate=pl.CostEstimate(flops=2 * total, bytes_accessed=5 * total, transcendentals=0),
    )(sq, *pieces, anchor, momentum)


def on_device(inner, anchor, momentum):
    inner = inner[0]
    rows, width = anchor.shape[1:]
    islands = lax.axis_size("island")
    entries = rows * 8 * width
    order = []

    def turn(value):
        return lax.optimization_barrier((value, order[-1]))[0] if order else value

    def note(value):
        order.append(value)
        return value

    send, keep = pick(inner)
    got_send, got_keep = hop(send, CORE), hop(keep, CORE)
    diff_send, base_send = differ(False, inner, anchor)
    send = note(diff_send + (base_send - got_send))
    diff_keep, base_keep = differ(True, turn(inner), anchor)
    a_r, bc_r = hop(send[:, :WA], Z), hop(send[:, WA:], X0)
    ab, c = in_vmem(first_kernel, (WA + WB, width - WA - WB), diff_keep, base_keep, got_keep, a_r, bc_r)
    c_r, ab_r = hop(c, Z), hop(ab, X1)
    a, b, c = in_vmem(second_kernel, (WA, WB, width - WA - WB), ab, c, ab_r, c_r)
    b_r, a_r, c_r = hop(b, Z), hop(a, X0), hop(c, X1)
    near, bc, sq = total(a, b, c, a_r, b_r, c_r)
    note(sq)
    a_far, bc_far = hop(near[:, :WA], Z), hop(bc, X0)
    for k, step in enumerate(STEPS):
        if k == 1:
            near_peer = hop(turn(near), CORE)
        if k == 4:
            far = jnp.concatenate([turn(v) for v in (a_far, bc_far)], axis=1)
            far_peer = hop(far, CORE)
            note(far)
        sq = note(sq + turn(hop(turn(sq), *step)))
    return tuple(update(sq, [near, near_peer, far, far_peer], anchor, momentum, entries, islands))


STEPS = (*FSDP_STEPS, (CORE, "island"), (ZX, "island"))


def solution(mesh):
    spec = P(None, "fsdp", None)
    return jax.shard_map(
        on_device,
        mesh=mesh,
        in_specs=(P("island", None, "fsdp", None), spec, spec),
        out_specs=(spec, spec),
        check_vma=False,
    )
```

```python
import jax
import jax.numpy as jnp
from jax import lax
from jax.sharding import PartitionSpec as P
from jax.experimental import pallas as pl
from jax.experimental.pallas import tpu as pltpu

EPS = 1e-06
RMS_MAX = 0.5
MU = 0.9
LR = 0.7
X, CORES = 4, 2


def island_id(z, x, core):
    return ((z % 2) * X + x % X) * CORES + core % CORES


def neighbour(x, core, parity):
    return x + 1 if (x + core + parity) % 2 == 0 else x - 1


PLACES = [(z, x, core) for z in range(2) for x in range(X) for core in range(CORES)]
CORE = [(island_id(*p), island_id(p[0], p[1], p[2] + 1)) for p in PLACES]
Z = [(island_id(*p), island_id(p[0] + 1, p[1], p[2])) for p in PLACES]
X0 = [(island_id(*p), island_id(p[0], neighbour(p[1], p[2], 0), p[2])) for p in PLACES]
X1 = [(island_id(*p), island_id(p[0], neighbour(p[1], p[2], 1), p[2])) for p in PLACES]
YZ = [(y, h) for y in range(4) for h in range(2)]
Y0 = [(y * 2 + h, (y ^ 1) * 2 + h) for y, h in YZ]
Y1 = [(y * 2 + h, ((y + (1 if y % 2 else -1)) % 4) * 2 + h) for y, h in YZ]
ZZ = [
    (island_id(z, x, core) * 8 + y * 2 + h, island_id(z + 1, x, core) * 8 + y * 2 + 1 - h)
    for z, x, core in PLACES
    for y, h in YZ
]


def hop(value, pairs, axis="island"):
    return lax.ppermute(value, axis, pairs)


WA, WB = 3456, 3456
VMEM = pl.BlockSpec(memory_space=pltpu.VMEM)
SMEM = pl.BlockSpec(memory_space=pltpu.SMEM)
HBM = pl.BlockSpec(memory_space=pltpu.HBM)


def diagonal():
    pairs = []
    for z, x, core in PLACES:
        pairs.append((island_id(z, x, core), island_id(z + 1, x + 2, core)))
    return pairs


ZX = diagonal()
FSDP_STEPS = ((Y0, "fsdp"), (Y1, "fsdp"), (ZZ, ("island", "fsdp")))


def position():
    me = lax.axis_index("island")
    core, x, z = me & 1, (me >> 1) & (X - 1), me >> 3
    return core, z, ((x + 1 - core) >> 1) & 1, ((x + core) >> 1) & 1


def fragments(mine, kept):
    core, z, bit, peer_bit = position()
    flip = 0 if kept else 1
    if mine:
        return 2 * core + (z ^ flip), 2 * core + (bit ^ flip)
    return 2 * (1 - core) + (z ^ flip), 2 * (1 - core) + (peer_bit ^ flip)


def fetches(source, target, frags, sem):
    rows, width = source.shape[1:]
    copies = []
    for k in range(rows // 8):
        for j, (lo, size) in enumerate(((0, WA), (WA, width - WA))):
            block = (pl.ds(8 * k, 8), pl.ds(lo, size))
            copies.append(pltpu.make_async_copy(source.at[(frags[j], *block)], target.at[block], sem.at[2 * k + j]))
    return copies


def run(copies):
    for copy in copies:
        copy.start()
    for copy in copies:
        copy.wait()


def subtract(base, diff):
    for start in range(0, diff.shape[1], 128):
        cols = slice(start, start + 128)
        diff[:, cols] = base[:, cols] - diff[:, cols]


def pick_kernel(inner, send, sem):
    run(fetches(inner, send, fragments(False, False), sem.at[0]))


def send_kernel(inner, anchor, diff, base, keep, sem):
    frags = fragments(True, False)
    kept = fetches(inner, keep, fragments(False, True), sem.at[2])
    copies = fetches(inner, diff, frags, sem.at[0]) + fetches(anchor, base, frags, sem.at[1])
    for copy in copies + kept:
        copy.start()
    for copy in copies:
        copy.wait()
    subtract(base, diff)
    for copy in kept:
        copy.wait()


def keep_kernel(inner, anchor, diff, base, sem):
    frags = fragments(True, True)
    run(fetches(inner, diff, frags, sem.at[0]) + fetches(anchor, base, frags, sem.at[1]))
    subtract(base, diff)


def fetch(kernel, count, mib, *arrays):
    rows, width = arrays[0].shape[1:]
    shape = jax.ShapeDtypeStruct((rows, width), jnp.float32)
    return pl.pallas_call(
        kernel,
        out_shape=(shape,) * count,
        in_specs=[HBM] * len(arrays),
        out_specs=(VMEM,) * count,
        scratch_shapes=[pltpu.SemaphoreType.DMA((3, 8))],
        compiler_params=pltpu.CompilerParams(vmem_limit_bytes=mib << 20),
        cost_estimate=pl.CostEstimate(flops=0, bytes_accessed=1024, transcendentals=0),
    )(*arrays)


def first_kernel(diff, base, got, a_r, bc_r, ab, c):
    for start in range(0, diff.shape[1], 128):
        cols = slice(start, start + 128)
        far = a_r[:, cols] if start < WA else bc_r[:, start - WA : start - WA + 128]
        value = diff[:, cols] + (base[:, cols] - got[:, cols]) + far
        if start < WA + WB:
            ab[:, cols] = value
        else:
            c[:, start - WA - WB : start - WA - WB + 128] = value


def second_kernel(ab, c, ab_r, c_r, a_out, b_out, c_out):
    for start in range(0, ab.shape[1], 128):
        cols = slice(start, start + 128)
        out, at = (a_out, start) if start < WA else (b_out, start - WA)
        out[:, at : at + 128] = ab[:, cols] + ab_r[:, cols]
    c_out[...] = c[...] + c_r[...]


def in_vmem(kernel, widths, *arrays):
    shapes = [jax.ShapeDtypeStruct((arrays[0].shape[0], w), jnp.float32) for w in widths]
    return pl.pallas_call(
        kernel,
        out_shape=tuple(shapes),
        in_specs=[VMEM] * len(arrays),
        out_specs=(VMEM,) * len(widths),
        compiler_params=pltpu.CompilerParams(vmem_limit_bytes=16 << 20),
        cost_estimate=pl.CostEstimate(flops=0, bytes_accessed=1024, transcendentals=0),
    )(*arrays)


def total_kernel(a, b, c, a_r, b_r, c_r, near, bc, sq):
    frags = fragments(True, True)
    sums = []
    for mine, got, lo in ((a, a_r, 0), (b, b_r, WA), (c, c_r, WA + WB)):
        size = mine.shape[1]
        part = jnp.zeros((mine.shape[0], 128), jnp.float32)
        for start in range(0, size, 128):
            value = mine[:, start : start + 128] + got[:, start : start + 128]
            near[:, lo + start : lo + start + 128] = value
            if lo:
                bc[:, lo - WA + start : lo - WA + start + 128] = value
            part = part + value * value
        sums.append(part)
    row = lax.broadcasted_iota(jnp.int32, (8, 128), 0)
    left, right = jnp.sum(sums[0]), jnp.sum(sums[1] + sums[2])
    sq[...] = jnp.where(row == frags[0], left, 0.0) + jnp.where(row == frags[1], right, 0.0)


def total(*pieces):
    rows = pieces[0].shape[0]
    width = sum(p.shape[1] for p in pieces[:3])
    shape = lambda *dims: jax.ShapeDtypeStruct(dims, jnp.float32)
    return pl.pallas_call(
        total_kernel,
        out_shape=(shape(rows, width), shape(rows, width - WA), shape(8, 128)),
        in_specs=[VMEM] * 6,
        out_specs=(VMEM,) * 3,
        compiler_params=pltpu.CompilerParams(vmem_limit_bytes=12 << 20),
        cost_estimate=pl.CostEstimate(flops=0, bytes_accessed=1024, transcendentals=0),
    )(*pieces)


def update_kernel(entries, islands, sq, *refs):
    sums, (anchor, momentum, out_a, out_m, va, vm, sem_in, sem_out) = refs[:4], refs[4:]
    width = anchor.shape[2]
    frags = [fragments(*which) for which in ((True, True), (False, True), (True, False), (False, False))]
    chunks = []
    for i in range(4):
        for j, (lo, hi) in enumerate(((0, WA), (WA, width))):
            chunks.append((i, frags[i][j], lo, hi - lo))

    def loads(n):
        i, frag, start, size = chunks[n]
        cols = pl.ds(start, size)
        return [
            pltpu.make_async_copy(anchor.at[frag, :, cols], va.at[i, :, cols], sem_in.at[0, n]),
            pltpu.make_async_copy(momentum.at[frag, :, cols], vm.at[i, :, cols], sem_in.at[1, n]),
        ]

    def stores(n):
        i, frag, start, size = chunks[n]
        cols = pl.ds(start, size)
        return [
            pltpu.make_async_copy(va.at[i, :, cols], out_a.at[frag, :, cols], sem_out.at[0, n]),
            pltpu.make_async_copy(vm.at[i, :, cols], out_m.at[frag, :, cols], sem_out.at[1, n]),
        ]

    for n in range(len(chunks)):
        for copy in loads(n):
            copy.start()
    for n, (i, frag, start, size) in enumerate(chunks):
        mean_sq = jnp.broadcast_to(sq[pl.ds(frag, 1), :], (8, 128)) * (1.0 / (islands * islands)) / entries
        factor = jnp.minimum(1.0, RMS_MAX / jnp.sqrt(mean_sq + EPS)) / islands
        for copy in loads(n):
            copy.wait()
        for at in range(start, start + size, 128):
            for row in range(0, 32, 8):
                block = (slice(row, row + 8), slice(at, at + 128))
                clipped = sums[i][block] * factor
                new_m = MU * vm[(i, *block)] + clipped
                va[(i, *block)] = va[(i, *block)] - LR * (clipped + MU * new_m)
                vm[(i, *block)] = new_m
        for copy in stores(n):
            copy.start()
    for n in range(len(chunks)):
        for copy in stores(n):
            copy.wait()


def update(sq, pieces, anchor, momentum, entries, islands):
    shape = jax.ShapeDtypeStruct(anchor.shape, anchor.dtype)
    total = anchor.size * 4
    any_spec = pl.BlockSpec(memory_space=pl.ANY)
    return pl.pallas_call(
        lambda *refs: update_kernel(entries, islands, *refs),
        out_shape=(shape, shape),
        in_specs=[VMEM] * 5 + [any_spec] * 2,
        out_specs=(HBM, HBM),
        scratch_shapes=[pltpu.VMEM(anchor.shape, jnp.float32)] * 2 + [pltpu.SemaphoreType.DMA((2, 8))] * 2,
        compiler_params=pltpu.CompilerParams(vmem_limit_bytes=40 << 20),
        cost_estimate=pl.CostEstimate(flops=2 * total, bytes_accessed=5 * total, transcendentals=0),
    )(sq, *pieces, anchor, momentum)


def on_device(inner, anchor, momentum):
    inner = inner[0]
    rows, width = anchor.shape[1:]
    islands = lax.axis_size("island")
    entries = rows * 8 * width
    order = []

    def turn(value):
        return lax.optimization_barrier((value, order[-1]))[0] if order else value

    def note(value):
        order.append(value)
        return value

    (send,) = fetch(pick_kernel, 1, 48, inner)
    got_send = hop(send, CORE)
    diff_send, base_send, keep = fetch(send_kernel, 3, 46, inner, anchor)
    got_keep = hop(keep, CORE)
    send = note(diff_send + (base_send - got_send))
    diff_keep, base_keep = fetch(keep_kernel, 2, 50, turn(inner), anchor)
    a_r, bc_r = hop(send[:, :WA], Z), hop(send[:, WA:], X0)
    ab, c = in_vmem(first_kernel, (WA + WB, width - WA - WB), diff_keep, base_keep, got_keep, a_r, bc_r)
    c_r, ab_r = hop(c, Z), hop(ab, X1)
    a, b, c = in_vmem(second_kernel, (WA, WB, width - WA - WB), ab, c, ab_r, c_r)
    b_r, a_r, c_r = hop(b, Z), hop(a, X0), hop(c, X1)
    near, bc, sq = total(a, b, c, a_r, b_r, c_r)
    note(sq)
    a_far, bc_far = hop(near[:, :WA], Z), hop(bc, X0)
    for k, step in enumerate(STEPS):
        if k == 1:
            near_peer = hop(turn(near), CORE)
        if k == 4:
            far = jnp.concatenate([turn(v) for v in (a_far, bc_far)], axis=1)
            far_peer = hop(far, CORE)
            note(far)
        sq = note(sq + turn(hop(turn(sq), *step)))
    return tuple(update(sq, [near, near_peer, far, far_peer], anchor, momentum, entries, islands))


STEPS = (*FSDP_STEPS, (CORE, "island"), (ZX, "island"))


def solution(mesh):
    spec = P(None, "fsdp", None)
    return jax.shard_map(
        on_device,
        mesh=mesh,
        in_specs=(P("island", None, "fsdp", None), spec, spec),
        out_specs=(spec, spec),
        check_vma=False,
    )
```

```python
import jax
import jax.numpy as jnp
from jax import lax
from jax.sharding import PartitionSpec as P
from jax.experimental import pallas as pl
from jax.experimental.pallas import tpu as pltpu

EPS = 1e-06
RMS_MAX = 0.5
MU = 0.9
LR = 0.7
X, CORES = 4, 2


def island_id(z, x, core):
    return ((z % 2) * X + x % X) * CORES + core % CORES


def neighbour(x, core, parity):
    return x + 1 if (x + core + parity) % 2 == 0 else x - 1


PLACES = [(z, x, core) for z in range(2) for x in range(X) for core in range(CORES)]
CORE = [(island_id(*p), island_id(p[0], p[1], p[2] + 1)) for p in PLACES]
Z = [(island_id(*p), island_id(p[0] + 1, p[1], p[2])) for p in PLACES]
X0 = [(island_id(*p), island_id(p[0], neighbour(p[1], p[2], 0), p[2])) for p in PLACES]
X1 = [(island_id(*p), island_id(p[0], neighbour(p[1], p[2], 1), p[2])) for p in PLACES]
YZ = [(y, h) for y in range(4) for h in range(2)]
Y0 = [(y * 2 + h, (y ^ 1) * 2 + h) for y, h in YZ]
Y1 = [(y * 2 + h, ((y + (1 if y % 2 else -1)) % 4) * 2 + h) for y, h in YZ]
ZZ = [
    (island_id(z, x, core) * 8 + y * 2 + h, island_id(z + 1, x, core) * 8 + y * 2 + 1 - h)
    for z, x, core in PLACES
    for y, h in YZ
]


def hop(value, pairs, axis="island"):
    return lax.ppermute(value, axis, pairs)


WA, WB = 3328, 3584
VMEM = pl.BlockSpec(memory_space=pltpu.VMEM)
SMEM = pl.BlockSpec(memory_space=pltpu.SMEM)
HBM = pl.BlockSpec(memory_space=pltpu.HBM)


def diagonal():
    pairs = []
    for z, x, core in PLACES:
        pairs.append((island_id(z, x, core), island_id(z + 1, neighbour(x, core, 0), core)))
    return pairs


ZX = diagonal()
FSDP_STEPS = ((Y0, "fsdp"), (Y1, "fsdp"), (ZZ, ("island", "fsdp")))


def position():
    me = lax.axis_index("island")
    core, x, z = me & 1, (me >> 1) & (X - 1), me >> 3
    return core, z, ((x + 1 - core) >> 1) & 1, ((x + core) >> 1) & 1


def fragments(mine, kept):
    core, z, bit, peer_bit = position()
    flip = 0 if kept else 1
    if mine:
        return 2 * core + (z ^ flip), 2 * core + (bit ^ flip)
    return 2 * (1 - core) + (z ^ flip), 2 * (1 - core) + (peer_bit ^ flip)


def fetches(source, target, frags, sem):
    rows, width = source.shape[1:]
    copies = []
    for k in range(rows // 8):
        for j, (lo, size) in enumerate(((0, WA), (WA, width - WA))):
            block = (pl.ds(8 * k, 8), pl.ds(lo, size))
            copies.append(pltpu.make_async_copy(source.at[(frags[j], *block)], target.at[block], sem.at[2 * k + j]))
    return copies


def run(copies):
    for copy in copies:
        copy.start()
    for copy in copies:
        copy.wait()


def subtract(base, diff):
    for start in range(0, diff.shape[1], 128):
        cols = slice(start, start + 128)
        diff[:, cols] = base[:, cols] - diff[:, cols]


def pick_kernel(inner, send, sem):
    run(fetches(inner, send, fragments(False, False), sem.at[0]))


def send_kernel(inner, anchor, diff, base, keep, sem):
    frags = fragments(True, False)
    kept = fetches(inner, keep, fragments(False, True), sem.at[2])
    copies = fetches(inner, diff, frags, sem.at[0]) + fetches(anchor, base, frags, sem.at[1])
    for copy in copies + kept:
        copy.start()
    for copy in copies:
        copy.wait()
    subtract(base, diff)
    for copy in kept:
        copy.wait()


def keep_kernel(inner, anchor, diff, base, sem):
    frags = fragments(True, True)
    run(fetches(inner, diff, frags, sem.at[0]) + fetches(anchor, base, frags, sem.at[1]))
    subtract(base, diff)


def fetch(kernel, count, mib, *arrays):
    rows, width = arrays[0].shape[1:]
    shape = jax.ShapeDtypeStruct((rows, width), jnp.float32)
    return pl.pallas_call(
        kernel,
        out_shape=(shape,) * count,
        in_specs=[HBM] * len(arrays),
        out_specs=(VMEM,) * count,
        scratch_shapes=[pltpu.SemaphoreType.DMA((3, 8))],
        compiler_params=pltpu.CompilerParams(vmem_limit_bytes=mib << 20),
        cost_estimate=pl.CostEstimate(flops=0, bytes_accessed=1024, transcendentals=0),
    )(*arrays)


def first_kernel(diff, base, got, a_r, bc_r, ab, c):
    for start in range(0, diff.shape[1], 128):
        cols = slice(start, start + 128)
        far = a_r[:, cols] if start < WA else bc_r[:, start - WA : start - WA + 128]
        value = diff[:, cols] + (base[:, cols] - got[:, cols]) + far
        if start < WA + WB:
            ab[:, cols] = value
        else:
            c[:, start - WA - WB : start - WA - WB + 128] = value


def second_kernel(ab, c, ab_r, c_r, a_out, b_out, c_out):
    for start in range(0, ab.shape[1], 128):
        cols = slice(start, start + 128)
        out, at = (a_out, start) if start < WA else (b_out, start - WA)
        out[:, at : at + 128] = ab[:, cols] + ab_r[:, cols]
    c_out[...] = c[...] + c_r[...]


def in_vmem(kernel, widths, *arrays):
    shapes = [jax.ShapeDtypeStruct((arrays[0].shape[0], w), jnp.float32) for w in widths]
    return pl.pallas_call(
        kernel,
        out_shape=tuple(shapes),
        in_specs=[VMEM] * len(arrays),
        out_specs=(VMEM,) * len(widths),
        compiler_params=pltpu.CompilerParams(vmem_limit_bytes=16 << 20),
        cost_estimate=pl.CostEstimate(flops=0, bytes_accessed=1024, transcendentals=0),
    )(*arrays)


def total_kernel(a, b, c, a_r, b_r, c_r, near, bc, sq):
    frags = fragments(True, True)
    sums = []
    for mine, got, lo in ((a, a_r, 0), (b, b_r, WA), (c, c_r, WA + WB)):
        size = mine.shape[1]
        part = jnp.zeros((mine.shape[0], 128), jnp.float32)
        for start in range(0, size, 128):
            value = mine[:, start : start + 128] + got[:, start : start + 128]
            near[:, lo + start : lo + start + 128] = value
            if lo:
                bc[:, lo - WA + start : lo - WA + start + 128] = value
            part = part + value * value
        sums.append(part)
    row = lax.broadcasted_iota(jnp.int32, (8, 128), 0)
    left, right = jnp.sum(sums[0]), jnp.sum(sums[1] + sums[2])
    sq[...] = jnp.where(row == frags[0], left, 0.0) + jnp.where(row == frags[1], right, 0.0)


def total(*pieces):
    rows = pieces[0].shape[0]
    width = sum(p.shape[1] for p in pieces[:3])
    shape = lambda *dims: jax.ShapeDtypeStruct(dims, jnp.float32)
    return pl.pallas_call(
        total_kernel,
        out_shape=(shape(rows, width), shape(rows, width - WA), shape(8, 128)),
        in_specs=[VMEM] * 6,
        out_specs=(VMEM,) * 3,
        compiler_params=pltpu.CompilerParams(vmem_limit_bytes=12 << 20),
        cost_estimate=pl.CostEstimate(flops=0, bytes_accessed=1024, transcendentals=0),
    )(*pieces)


def update_kernel(entries, islands, sq, *refs):
    sums, (anchor, momentum, out_a, out_m, va, vm, sem_in, sem_out) = refs[:4], refs[4:]
    width = anchor.shape[2]
    frags = [fragments(*which) for which in ((True, True), (False, True), (True, False), (False, False))]
    chunks = []
    for i in range(4):
        for j, (lo, hi) in enumerate(((0, WA), (WA, width))):
            chunks.append((i, frags[i][j], lo, hi - lo))

    def loads(n):
        i, frag, start, size = chunks[n]
        cols = pl.ds(start, size)
        return [
            pltpu.make_async_copy(anchor.at[frag, :, cols], va.at[i, :, cols], sem_in.at[0, n]),
            pltpu.make_async_copy(momentum.at[frag, :, cols], vm.at[i, :, cols], sem_in.at[1, n]),
        ]

    def stores(n):
        i, frag, start, size = chunks[n]
        cols = pl.ds(start, size)
        return [
            pltpu.make_async_copy(va.at[i, :, cols], out_a.at[frag, :, cols], sem_out.at[0, n]),
            pltpu.make_async_copy(vm.at[i, :, cols], out_m.at[frag, :, cols], sem_out.at[1, n]),
        ]

    for n in range(len(chunks)):
        for copy in loads(n):
            copy.start()
    for n, (i, frag, start, size) in enumerate(chunks):
        mean_sq = jnp.broadcast_to(sq[pl.ds(frag, 1), :], (8, 128)) * (1.0 / (islands * islands)) / entries
        factor = jnp.minimum(1.0, RMS_MAX / jnp.sqrt(mean_sq + EPS)) / islands
        for copy in loads(n):
            copy.wait()
        for at in range(start, start + size, 128):
            for row in range(0, 32, 8):
                block = (slice(row, row + 8), slice(at, at + 128))
                clipped = sums[i][block] * factor
                new_m = MU * vm[(i, *block)] + clipped
                va[(i, *block)] = va[(i, *block)] - LR * (clipped + MU * new_m)
                vm[(i, *block)] = new_m
        for copy in stores(n):
            copy.start()
    for n in range(len(chunks)):
        for copy in stores(n):
            copy.wait()


def update(sq, pieces, anchor, momentum, entries, islands):
    shape = jax.ShapeDtypeStruct(anchor.shape, anchor.dtype)
    total = anchor.size * 4
    any_spec = pl.BlockSpec(memory_space=pl.ANY)
    return pl.pallas_call(
        lambda *refs: update_kernel(entries, islands, *refs),
        out_shape=(shape, shape),
        in_specs=[VMEM] * 5 + [any_spec] * 2,
        out_specs=(HBM, HBM),
        scratch_shapes=[pltpu.VMEM(anchor.shape, jnp.float32)] * 2 + [pltpu.SemaphoreType.DMA((2, 8))] * 2,
        compiler_params=pltpu.CompilerParams(vmem_limit_bytes=40 << 20),
        cost_estimate=pl.CostEstimate(flops=2 * total, bytes_accessed=5 * total, transcendentals=0),
    )(sq, *pieces, anchor, momentum)


def on_device(inner, anchor, momentum):
    inner = inner[0]
    rows, width = anchor.shape[1:]
    islands = lax.axis_size("island")
    entries = rows * 8 * width
    order = []

    def turn(value):
        return lax.optimization_barrier((value, order[-1]))[0] if order else value

    def note(value):
        order.append(value)
        return value

    (send,) = fetch(pick_kernel, 1, 48, inner)
    got_send = hop(send, CORE)
    diff_send, base_send, keep = fetch(send_kernel, 3, 46, inner, anchor)
    got_keep = hop(keep, CORE)
    send = note(diff_send + (base_send - got_send))
    diff_keep, base_keep = fetch(keep_kernel, 2, 50, turn(inner), anchor)
    a_r, bc_r = hop(send[:, :WA], Z), hop(send[:, WA:], X0)
    ab, c = in_vmem(first_kernel, (WA + WB, width - WA - WB), diff_keep, base_keep, got_keep, a_r, bc_r)
    c_r, ab_r = hop(c, Z), hop(ab, X1)
    a, b, c = in_vmem(second_kernel, (WA, WB, width - WA - WB), ab, c, ab_r, c_r)
    b_r, a_r, c_r = hop(b, Z), hop(a, X0), hop(c, X1)
    near, bc, sq = total(a, b, c, a_r, b_r, c_r)
    note(sq)
    a_far, bc_far = hop(near[:, :WA], Z), hop(bc, X0)
    for k, step in enumerate(STEPS):
        if k == 1:
            near_peer = hop(turn(near), CORE)
        if k == 3:
            far = jnp.concatenate([turn(v) for v in (a_far, bc_far)], axis=1)
            far_peer = hop(far, CORE)
            note(far)
        sq = note(sq + turn(hop(turn(sq), *step)))
    return tuple(update(sq, [near, near_peer, far, far_peer], anchor, momentum, entries, islands))


STEPS = (*FSDP_STEPS, (ZX, "island"), (CORE, "island"))


def solution(mesh):
    spec = P(None, "fsdp", None)
    return jax.shard_map(
        on_device,
        mesh=mesh,
        in_specs=(P("island", None, "fsdp", None), spec, spec),
        out_specs=(spec, spec),
        check_vma=False,
    )
```

```python
import jax
import jax.numpy as jnp
from jax import lax
from jax.sharding import PartitionSpec as P
from jax.experimental import pallas as pl
from jax.experimental.pallas import tpu as pltpu

EPS = 1e-06
RMS_MAX = 0.5
MU = 0.9
LR = 0.7
X, CORES = 4, 2


def island_id(z, x, core):
    return ((z % 2) * X + x % X) * CORES + core % CORES


def neighbour(x, core, parity):
    return x + 1 if (x + core + parity) % 2 == 0 else x - 1


PLACES = [(z, x, core) for z in range(2) for x in range(X) for core in range(CORES)]
CORE = [(island_id(*p), island_id(p[0], p[1], p[2] + 1)) for p in PLACES]
Z = [(island_id(*p), island_id(p[0] + 1, p[1], p[2])) for p in PLACES]
X0 = [(island_id(*p), island_id(p[0], neighbour(p[1], p[2], 0), p[2])) for p in PLACES]
X1 = [(island_id(*p), island_id(p[0], neighbour(p[1], p[2], 1), p[2])) for p in PLACES]
YZ = [(y, h) for y in range(4) for h in range(2)]
Y0 = [(y * 2 + h, (y ^ 1) * 2 + h) for y, h in YZ]
Y1 = [(y * 2 + h, ((y + (1 if y % 2 else -1)) % 4) * 2 + h) for y, h in YZ]
ZZ = [
    (island_id(z, x, core) * 8 + y * 2 + h, island_id(z + 1, x, core) * 8 + y * 2 + 1 - h)
    for z, x, core in PLACES
    for y, h in YZ
]


def hop(value, pairs, axis="island"):
    return lax.ppermute(value, axis, pairs)


WA, WB = 3328, 3712
VMEM = pl.BlockSpec(memory_space=pltpu.VMEM)
SMEM = pl.BlockSpec(memory_space=pltpu.SMEM)
HBM = pl.BlockSpec(memory_space=pltpu.HBM)


def diagonal():
    pairs = []
    for z, x, core in PLACES:
        pairs.append((island_id(z, x, core), island_id(z + 1, neighbour(x, core, 0), core)))
    return pairs


ZX = diagonal()
FSDP_STEPS = ((Y0, "fsdp"), (Y1, "fsdp"), (ZZ, ("island", "fsdp")))


def position():
    me = lax.axis_index("island")
    core, x, z = me & 1, (me >> 1) & (X - 1), me >> 3
    return core, z, ((x + 1 - core) >> 1) & 1, ((x + core) >> 1) & 1


def fragments(mine, kept):
    core, z, bit, peer_bit = position()
    flip = 0 if kept else 1
    if mine:
        return 2 * core + (z ^ flip), 2 * core + (bit ^ flip)
    return 2 * (1 - core) + (z ^ flip), 2 * (1 - core) + (peer_bit ^ flip)


def fetches(source, target, frags, sem):
    rows, width = source.shape[1:]
    copies = []
    for k in range(rows // 8):
        for j, (lo, size) in enumerate(((0, WA), (WA, width - WA))):
            block = (pl.ds(8 * k, 8), pl.ds(lo, size))
            copies.append(pltpu.make_async_copy(source.at[(frags[j], *block)], target.at[block], sem.at[2 * k + j]))
    return copies


def run(copies):
    for copy in copies:
        copy.start()
    for copy in copies:
        copy.wait()


def subtract(base, diff):
    for start in range(0, diff.shape[1], 128):
        cols = slice(start, start + 128)
        diff[:, cols] = base[:, cols] - diff[:, cols]


def pick_kernel(inner, send, sem):
    run(fetches(inner, send, fragments(False, False), sem.at[0]))


def send_kernel(inner, anchor, diff, base, keep, sem):
    frags = fragments(True, False)
    kept = fetches(inner, keep, fragments(False, True), sem.at[2])
    copies = fetches(inner, diff, frags, sem.at[0]) + fetches(anchor, base, frags, sem.at[1])
    for copy in copies + kept:
        copy.start()
    for copy in copies:
        copy.wait()
    subtract(base, diff)
    for copy in kept:
        copy.wait()


def keep_kernel(inner, anchor, diff, base, sem):
    frags = fragments(True, True)
    run(fetches(inner, diff, frags, sem.at[0]) + fetches(anchor, base, frags, sem.at[1]))
    subtract(base, diff)


def fetch(kernel, count, mib, *arrays):
    rows, width = arrays[0].shape[1:]
    shape = jax.ShapeDtypeStruct((rows, width), jnp.float32)
    return pl.pallas_call(
        kernel,
        out_shape=(shape,) * count,
        in_specs=[HBM] * len(arrays),
        out_specs=(VMEM,) * count,
        scratch_shapes=[pltpu.SemaphoreType.DMA((3, 8))],
        compiler_params=pltpu.CompilerParams(vmem_limit_bytes=mib << 20),
        cost_estimate=pl.CostEstimate(flops=0, bytes_accessed=1024, transcendentals=0),
    )(*arrays)


def first_kernel(diff, base, got, a_r, bc_r, ab, c):
    for start in range(0, diff.shape[1], 128):
        cols = slice(start, start + 128)
        far = a_r[:, cols] if start < WA else bc_r[:, start - WA : start - WA + 128]
        value = diff[:, cols] + (base[:, cols] - got[:, cols]) + far
        if start < WA + WB:
            ab[:, cols] = value
        else:
            c[:, start - WA - WB : start - WA - WB + 128] = value


def second_kernel(ab, c, ab_r, c_r, a_out, b_out, c_out):
    for start in range(0, ab.shape[1], 128):
        cols = slice(start, start + 128)
        out, at = (a_out, start) if start < WA else (b_out, start - WA)
        out[:, at : at + 128] = ab[:, cols] + ab_r[:, cols]
    c_out[...] = c[...] + c_r[...]


def in_vmem(kernel, widths, *arrays):
    shapes = [jax.ShapeDtypeStruct((arrays[0].shape[0], w), jnp.float32) for w in widths]
    return pl.pallas_call(
        kernel,
        out_shape=tuple(shapes),
        in_specs=[VMEM] * len(arrays),
        out_specs=(VMEM,) * len(widths),
        compiler_params=pltpu.CompilerParams(vmem_limit_bytes=16 << 20),
        cost_estimate=pl.CostEstimate(flops=0, bytes_accessed=1024, transcendentals=0),
    )(*arrays)


def total_kernel(a, b, c, a_r, b_r, c_r, near, bc, sq):
    frags = fragments(True, True)
    sums = []
    for mine, got, lo in ((a, a_r, 0), (b, b_r, WA), (c, c_r, WA + WB)):
        size = mine.shape[1]
        part = jnp.zeros((mine.shape[0], 128), jnp.float32)
        for start in range(0, size, 128):
            value = mine[:, start : start + 128] + got[:, start : start + 128]
            near[:, lo + start : lo + start + 128] = value
            if lo:
                bc[:, lo - WA + start : lo - WA + start + 128] = value
            part = part + value * value
        sums.append(part)
    row = lax.broadcasted_iota(jnp.int32, (8, 128), 0)
    left, right = jnp.sum(sums[0]), jnp.sum(sums[1] + sums[2])
    sq[...] = jnp.where(row == frags[0], left, 0.0) + jnp.where(row == frags[1], right, 0.0)


def total(*pieces):
    rows = pieces[0].shape[0]
    width = sum(p.shape[1] for p in pieces[:3])
    shape = lambda *dims: jax.ShapeDtypeStruct(dims, jnp.float32)
    return pl.pallas_call(
        total_kernel,
        out_shape=(shape(rows, width), shape(rows, width - WA), shape(8, 128)),
        in_specs=[VMEM] * 6,
        out_specs=(VMEM,) * 3,
        compiler_params=pltpu.CompilerParams(vmem_limit_bytes=12 << 20),
        cost_estimate=pl.CostEstimate(flops=0, bytes_accessed=1024, transcendentals=0),
    )(*pieces)


def update_kernel(entries, islands, sq, *refs):
    sums, (anchor, momentum, out_a, out_m, va, vm, sem_in, sem_out) = refs[:4], refs[4:]
    width = anchor.shape[2]
    frags = [fragments(*which) for which in ((True, True), (False, True), (True, False), (False, False))]
    chunks = []
    for i in range(4):
        for j, (lo, hi) in enumerate(((0, WA), (WA, width))):
            chunks.append((i, frags[i][j], lo, hi - lo))

    def loads(n):
        i, frag, start, size = chunks[n]
        cols = pl.ds(start, size)
        return [
            pltpu.make_async_copy(anchor.at[frag, :, cols], va.at[i, :, cols], sem_in.at[0, n]),
            pltpu.make_async_copy(momentum.at[frag, :, cols], vm.at[i, :, cols], sem_in.at[1, n]),
        ]

    def stores(n):
        i, frag, start, size = chunks[n]
        cols = pl.ds(start, size)
        return [
            pltpu.make_async_copy(va.at[i, :, cols], out_a.at[frag, :, cols], sem_out.at[0, n]),
            pltpu.make_async_copy(vm.at[i, :, cols], out_m.at[frag, :, cols], sem_out.at[1, n]),
        ]

    for n in range(len(chunks)):
        for copy in loads(n):
            copy.start()
    for n, (i, frag, start, size) in enumerate(chunks):
        mean_sq = jnp.broadcast_to(sq[pl.ds(frag, 1), :], (8, 128)) * (1.0 / (islands * islands)) / entries
        factor = jnp.minimum(1.0, RMS_MAX / jnp.sqrt(mean_sq + EPS)) / islands
        for copy in loads(n):
            copy.wait()
        for at in range(start, start + size, 128):
            for row in range(0, 32, 8):
                block = (slice(row, row + 8), slice(at, at + 128))
                clipped = sums[i][block] * factor
                new_m = MU * vm[(i, *block)] + clipped
                va[(i, *block)] = va[(i, *block)] - LR * (clipped + MU * new_m)
                vm[(i, *block)] = new_m
        for copy in stores(n):
            copy.start()
    for n in range(len(chunks)):
        for copy in stores(n):
            copy.wait()


def update(sq, pieces, anchor, momentum, entries, islands):
    shape = jax.ShapeDtypeStruct(anchor.shape, anchor.dtype)
    total = anchor.size * 4
    any_spec = pl.BlockSpec(memory_space=pl.ANY)
    return pl.pallas_call(
        lambda *refs: update_kernel(entries, islands, *refs),
        out_shape=(shape, shape),
        in_specs=[VMEM] * 5 + [any_spec] * 2,
        out_specs=(HBM, HBM),
        scratch_shapes=[pltpu.VMEM(anchor.shape, jnp.float32)] * 2 + [pltpu.SemaphoreType.DMA((2, 8))] * 2,
        compiler_params=pltpu.CompilerParams(vmem_limit_bytes=40 << 20),
        cost_estimate=pl.CostEstimate(flops=2 * total, bytes_accessed=5 * total, transcendentals=0),
    )(sq, *pieces, anchor, momentum)


def on_device(inner, anchor, momentum):
    inner = inner[0]
    rows, width = anchor.shape[1:]
    islands = lax.axis_size("island")
    entries = rows * 8 * width
    order = []

    def turn(value):
        return lax.optimization_barrier((value, order[-1]))[0] if order else value

    def note(value):
        order.append(value)
        return value

    (send,) = fetch(pick_kernel, 1, 48, inner)
    got_send = hop(send, CORE)
    diff_send, base_send, keep = fetch(send_kernel, 3, 46, inner, anchor)
    got_keep = hop(keep, CORE)
    send = note(diff_send + (base_send - got_send))
    diff_keep, base_keep = fetch(keep_kernel, 2, 50, turn(inner), anchor)
    a_r, bc_r = hop(send[:, :WA], Z), hop(send[:, WA:], X0)
    ab, c = in_vmem(first_kernel, (WA + WB, width - WA - WB), diff_keep, base_keep, got_keep, a_r, bc_r)
    c_r, ab_r = hop(c, Z), hop(ab, X1)
    a, b, c = in_vmem(second_kernel, (WA, WB, width - WA - WB), ab, c, ab_r, c_r)
    b_r, a_r, c_r = hop(b, Z), hop(a, X0), hop(c, X1)
    near, bc, sq = total(a, b, c, a_r, b_r, c_r)
    note(sq)
    a_far, bc_far = hop(near[:, :WA], Z), hop(bc, X0)
    for k, step in enumerate(STEPS):
        if k == 3:
            near_peer = hop(turn(near), CORE)
            far = jnp.concatenate([turn(v) for v in (a_far, bc_far)], axis=1)
            far_peer = hop(far, CORE)
            note(far)
        sq = note(sq + turn(hop(turn(sq), *step)))
    return tuple(update(sq, [near, near_peer, far, far_peer], anchor, momentum, entries, islands))


STEPS = (*FSDP_STEPS, (ZX, "island"), (CORE, "island"))


def solution(mesh):
    spec = P(None, "fsdp", None)
    return jax.shard_map(
        on_device,
        mesh=mesh,
        in_specs=(P("island", None, "fsdp", None), spec, spec),
        out_specs=(spec, spec),
        check_vma=False,
    )
```

```python
import jax
import jax.numpy as jnp
from jax import lax
from jax.sharding import PartitionSpec as P
from jax.experimental import pallas as pl
from jax.experimental.pallas import tpu as pltpu

EPS = 1e-06
RMS_MAX = 0.5
MU = 0.9
LR = 0.7
X, CORES = 4, 2


def island_id(z, x, core):
    return ((z % 2) * X + x % X) * CORES + core % CORES


def neighbour(x, core, parity):
    return x + 1 if (x + core + parity) % 2 == 0 else x - 1


PLACES = [(z, x, core) for z in range(2) for x in range(X) for core in range(CORES)]
CORE = [(island_id(*p), island_id(p[0], p[1], p[2] + 1)) for p in PLACES]
Z = [(island_id(*p), island_id(p[0] + 1, p[1], p[2])) for p in PLACES]
X0 = [(island_id(*p), island_id(p[0], neighbour(p[1], p[2], 0), p[2])) for p in PLACES]
X1 = [(island_id(*p), island_id(p[0], neighbour(p[1], p[2], 1), p[2])) for p in PLACES]
YZ = [(y, h) for y in range(4) for h in range(2)]
Y0 = [(y * 2 + h, (y ^ 1) * 2 + h) for y, h in YZ]
Y1 = [(y * 2 + h, ((y + (1 if y % 2 else -1)) % 4) * 2 + h) for y, h in YZ]
ZZ = [
    (island_id(z, x, core) * 8 + y * 2 + h, island_id(z + 1, x, core) * 8 + y * 2 + 1 - h)
    for z, x, core in PLACES
    for y, h in YZ
]


def hop(value, pairs, axis="island"):
    return lax.ppermute(value, axis, pairs)


WA, WB = 3328, 3712
VMEM = pl.BlockSpec(memory_space=pltpu.VMEM)
SMEM = pl.BlockSpec(memory_space=pltpu.SMEM)
HBM = pl.BlockSpec(memory_space=pltpu.HBM)


def diagonal():
    pairs = []
    for z, x, core in PLACES:
        pairs.append((island_id(z, x, core), island_id(z + 1, neighbour(x, core, 0), core)))
    return pairs


ZX = diagonal()
FSDP_STEPS = ((Y0, "fsdp"), (Y1, "fsdp"), (ZZ, ("island", "fsdp")))


def position():
    me = lax.axis_index("island")
    core, x, z = me & 1, (me >> 1) & (X - 1), me >> 3
    return core, z, ((x + 1 - core) >> 1) & 1, ((x + core) >> 1) & 1


def fragments(mine, kept):
    core, z, bit, peer_bit = position()
    flip = 0 if kept else 1
    if mine:
        return 2 * core + (z ^ flip), 2 * core + (bit ^ flip)
    return 2 * (1 - core) + (z ^ flip), 2 * (1 - core) + (peer_bit ^ flip)


def fetches(source, target, frags, sem):
    rows, width = source.shape[1:]
    copies = []
    for k in range(rows // 8):
        for j, (lo, size) in enumerate(((0, WA), (WA, width - WA))):
            block = (pl.ds(8 * k, 8), pl.ds(lo, size))
            copies.append(pltpu.make_async_copy(source.at[(frags[j], *block)], target.at[block], sem.at[2 * k + j]))
    return copies


def run(copies):
    for copy in copies:
        copy.start()
    for copy in copies:
        copy.wait()


def subtract(base, diff):
    for start in range(0, diff.shape[1], 128):
        cols = slice(start, start + 128)
        diff[:, cols] = base[:, cols] - diff[:, cols]


def pick_kernel(inner, send, sem):
    run(fetches(inner, send, fragments(False, False), sem.at[0]))


def send_kernel(inner, anchor, diff, base, keep, sem):
    frags = fragments(True, False)
    kept = fetches(inner, keep, fragments(False, True), sem.at[2])
    copies = fetches(inner, diff, frags, sem.at[0]) + fetches(anchor, base, frags, sem.at[1])
    for copy in copies + kept:
        copy.start()
    for copy in copies:
        copy.wait()
    subtract(base, diff)
    for copy in kept:
        copy.wait()


def keep_kernel(inner, anchor, diff, base, sem):
    frags = fragments(True, True)
    run(fetches(inner, diff, frags, sem.at[0]) + fetches(anchor, base, frags, sem.at[1]))
    subtract(base, diff)


def fetch(kernel, count, mib, *arrays):
    rows, width = arrays[0].shape[1:]
    shape = jax.ShapeDtypeStruct((rows, width), jnp.float32)
    return pl.pallas_call(
        kernel,
        out_shape=(shape,) * count,
        in_specs=[HBM] * len(arrays),
        out_specs=(VMEM,) * count,
        scratch_shapes=[pltpu.SemaphoreType.DMA((3, 8))],
        compiler_params=pltpu.CompilerParams(vmem_limit_bytes=mib << 20),
        cost_estimate=pl.CostEstimate(flops=0, bytes_accessed=1024, transcendentals=0),
    )(*arrays)


def first_kernel(diff, base, got, a_r, bc_r, ab, c):
    for start in range(0, diff.shape[1], 128):
        cols = slice(start, start + 128)
        far = a_r[:, cols] if start < WA else bc_r[:, start - WA : start - WA + 128]
        value = diff[:, cols] + (base[:, cols] - got[:, cols]) + far
        if start < WA + WB:
            ab[:, cols] = value
        else:
            c[:, start - WA - WB : start - WA - WB + 128] = value


def second_kernel(ab, c, ab_r, c_r, a_out, b_out, c_out):
    for start in range(0, ab.shape[1], 128):
        cols = slice(start, start + 128)
        out, at = (a_out, start) if start < WA else (b_out, start - WA)
        out[:, at : at + 128] = ab[:, cols] + ab_r[:, cols]
    c_out[...] = c[...] + c_r[...]


def in_vmem(kernel, widths, *arrays):
    shapes = [jax.ShapeDtypeStruct((arrays[0].shape[0], w), jnp.float32) for w in widths]
    return pl.pallas_call(
        kernel,
        out_shape=tuple(shapes),
        in_specs=[VMEM] * len(arrays),
        out_specs=(VMEM,) * len(widths),
        compiler_params=pltpu.CompilerParams(vmem_limit_bytes=16 << 20),
        cost_estimate=pl.CostEstimate(flops=0, bytes_accessed=1024, transcendentals=0),
    )(*arrays)


def total_kernel(a, b, c, a_r, b_r, c_r, near, bc, sq):
    frags = fragments(True, True)
    sums = []
    for mine, got, lo in ((a, a_r, 0), (b, b_r, WA), (c, c_r, WA + WB)):
        size = mine.shape[1]
        part = jnp.zeros((mine.shape[0], 128), jnp.float32)
        for start in range(0, size, 128):
            value = mine[:, start : start + 128] + got[:, start : start + 128]
            near[:, lo + start : lo + start + 128] = value
            if lo:
                bc[:, lo - WA + start : lo - WA + start + 128] = value
            part = part + value * value
        sums.append(part)
    row = lax.broadcasted_iota(jnp.int32, (8, 128), 0)
    left, right = jnp.sum(sums[0]), jnp.sum(sums[1] + sums[2])
    sq[...] = jnp.where(row == frags[0], left, 0.0) + jnp.where(row == frags[1], right, 0.0)


def total(*pieces):
    rows = pieces[0].shape[0]
    width = sum(p.shape[1] for p in pieces[:3])
    shape = lambda *dims: jax.ShapeDtypeStruct(dims, jnp.float32)
    return pl.pallas_call(
        total_kernel,
        out_shape=(shape(rows, width), shape(rows, width - WA), shape(8, 128)),
        in_specs=[VMEM] * 6,
        out_specs=(VMEM,) * 3,
        compiler_params=pltpu.CompilerParams(vmem_limit_bytes=12 << 20),
        cost_estimate=pl.CostEstimate(flops=0, bytes_accessed=1024, transcendentals=0),
    )(*pieces)


def update_kernel(entries, islands, sq, *refs):
    sums, (anchor, momentum, out_a, out_m, va, vm, sem_in, sem_out) = refs[:4], refs[4:]
    width = anchor.shape[2]
    frags = [fragments(*which) for which in ((True, True), (False, True), (True, False), (False, False))]
    chunks = []
    for i in range(4):
        for j, (lo, hi) in enumerate(((0, WA), (WA, width))):
            chunks.append((i, frags[i][j], lo, hi - lo))

    def loads(n):
        i, frag, start, size = chunks[n]
        cols = pl.ds(start, size)
        return [
            pltpu.make_async_copy(anchor.at[frag, :, cols], va.at[i, :, cols], sem_in.at[0, n]),
            pltpu.make_async_copy(momentum.at[frag, :, cols], vm.at[i, :, cols], sem_in.at[1, n]),
        ]

    def stores(n):
        i, frag, start, size = chunks[n]
        cols = pl.ds(start, size)
        return [
            pltpu.make_async_copy(va.at[i, :, cols], out_a.at[frag, :, cols], sem_out.at[0, n]),
            pltpu.make_async_copy(vm.at[i, :, cols], out_m.at[frag, :, cols], sem_out.at[1, n]),
        ]

    for n in range(len(chunks)):
        for copy in loads(n):
            copy.start()
    for n, (i, frag, start, size) in enumerate(chunks):
        mean_sq = jnp.broadcast_to(sq[pl.ds(frag, 1), :], (8, 128)) * (1.0 / (islands * islands)) / entries
        factor = jnp.minimum(1.0, RMS_MAX / jnp.sqrt(mean_sq + EPS)) / islands
        for copy in loads(n):
            copy.wait()
        for at in range(start, start + size, 128):
            for row in range(0, 32, 8):
                block = (slice(row, row + 8), slice(at, at + 128))
                clipped = sums[i][block] * factor
                new_m = MU * vm[(i, *block)] + clipped
                va[(i, *block)] = va[(i, *block)] - LR * (clipped + MU * new_m)
                vm[(i, *block)] = new_m
        for copy in stores(n):
            copy.start()
    for n in range(len(chunks)):
        for copy in stores(n):
            copy.wait()


def update(sq, pieces, anchor, momentum, entries, islands):
    shape = jax.ShapeDtypeStruct(anchor.shape, anchor.dtype)
    total = anchor.size * 4
    any_spec = pl.BlockSpec(memory_space=pl.ANY)
    return pl.pallas_call(
        lambda *refs: update_kernel(entries, islands, *refs),
        out_shape=(shape, shape),
        in_specs=[VMEM] * 5 + [any_spec] * 2,
        out_specs=(HBM, HBM),
        scratch_shapes=[pltpu.VMEM(anchor.shape, jnp.float32)] * 2 + [pltpu.SemaphoreType.DMA((2, 8))] * 2,
        compiler_params=pltpu.CompilerParams(vmem_limit_bytes=40 << 20),
        cost_estimate=pl.CostEstimate(flops=2 * total, bytes_accessed=5 * total, transcendentals=0),
    )(sq, *pieces, anchor, momentum)


def on_device(inner, anchor, momentum):
    inner = inner[0]
    rows, width = anchor.shape[1:]
    islands = lax.axis_size("island")
    entries = rows * 8 * width
    order = []

    def turn(value):
        return lax.optimization_barrier((value, order[-1]))[0] if order else value

    def note(value):
        order.append(value)
        return value

    (send,) = fetch(pick_kernel, 1, 48, inner)
    got_send = hop(send, CORE)
    diff_send, base_send, keep = fetch(send_kernel, 3, 46, inner, anchor)
    got_keep = hop(keep, CORE)
    send = note(diff_send + (base_send - got_send))
    diff_keep, base_keep = fetch(keep_kernel, 2, 50, turn(inner), anchor)
    a_r, bc_r = hop(send[:, :WA], Z), hop(send[:, WA:], X0)
    ab, c = in_vmem(first_kernel, (WA + WB, width - WA - WB), diff_keep, base_keep, got_keep, a_r, bc_r)
    c_r, ab_r = hop(c, Z), hop(ab, X1)
    a, b, c = in_vmem(second_kernel, (WA, WB, width - WA - WB), ab, c, ab_r, c_r)
    b_r, a_r, c_r = hop(b, Z), hop(a, X0), hop(c, X1)
    near, bc, sq = total(a, b, c, a_r, b_r, c_r)
    note(sq)
    a_far, bc_far = hop(near[:, :WA], Z), hop(bc, X0)
    for k, step in enumerate(STEPS):
        if k == 3:
            near_peer = hop(turn(near), CORE)
            far = jnp.concatenate([turn(v) for v in (a_far, bc_far)], axis=1)
            far_peer = hop(far, CORE)
            note(far)
        sq = note(sq + turn(hop(turn(sq), *step)))
    return tuple(update(sq, [near, near_peer, far, far_peer], anchor, momentum, entries, islands))


STEPS = (FSDP_STEPS[2], *FSDP_STEPS[:2], (ZX, "island"), (CORE, "island"))


def solution(mesh):
    spec = P(None, "fsdp", None)
    return jax.shard_map(
        on_device,
        mesh=mesh,
        in_specs=(P("island", None, "fsdp", None), spec, spec),
        out_specs=(spec, spec),
        check_vma=False,
    )
```
